32 devices in a mesh: dp: 2 (over x), expert: 16 (over z, y, core).
Axes of the slice: x: 2, y: 2, z: 4, core: 2. Of those that a mesh axis runs over, the one named last changes fastest.
Arguments:
- tokens: bfloat16 [768, 1024], P(('dp', 'expert')), may hold values from -6 to 6
- grad_out: bfloat16 [768, 1024], P(('dp', 'expert')), may hold values from -6 to 6
- expert_ids: int32 [768, 8], P(('dp', 'expert')), may hold values from 0 to 15, all different within a row; in each aligned block of 24 rows (0 to 23, 24 to 47, ...) at most 18 rows name the same one
- gates: float32 [768, 8], P(('dp', 'expert')), may hold values from 0.05 to 0.5
- w_in: bfloat16 [16, 1024, 2, 512], P('expert', None, None, 'dp'), may hold values from -0.1875 to 0.1875
- w_out: bfloat16 [16, 512, 1024], P('expert', 'dp'), may hold values from -0.25 to 0.25
Outputs:
- mixed: bfloat16 [768, 1024], P(('dp', 'expert'))
- grad_tokens: bfloat16 [768, 1024], P(('dp', 'expert'))
- grad_gates: float32 [768, 8], P(('dp', 'expert'))
- grad_w_in: float32 [16, 1024, 2, 512], P('expert', None, None, 'dp')
- grad_w_out: float32 [16, 512, 1024], P('expert', 'dp')
The draws below stay inside these ranges and needn't reach their ends.
Inputs may be any that keep to these rules, and one draw needn't show every extreme that they name: `expert_ids`: each token names 8 different experts; the rows of one device name no expert more than 18 times, a bound that some block reaches.
All inputs are finite; a program needn't handle non-finite values.
Results may differ from the reference program's by a relative error of at most 0.012.
Values may be sent and summed in bfloat16 or wider, within the bound.
A program may use at most 64 MiB of HBM per device.

```python
import math
import jax
import jax.numpy as jnp
import numpy as np
from jax import lax

D = 1024
H = 512
TOP = 8
TOK_DEV = 24
EXPERTS = 16
CAP = 18
TOKENS = 768
N_DP = 2
N_EXPERT = 16


def shard_levels(rng, shape, shards, low, high):
    factor_of = 1.0
    for dim, parts in shards:
        heights = jax.random.uniform(jax.random.fold_in(jax.random.fold_in(rng, 6), dim), (parts,), jnp.float32, low / len(shards), high / len(shards))
        factor_of = factor_of * jnp.repeat(jnp.exp(heights), shape[dim] // parts).reshape((-1,) + (1,) * (len(shape) - 1 - dim))
    return factor_of


def shared_out(rng, own, number, rows, number_of, top, limit, lean):
    order = jax.random.permutation(rng, number_of)
    crowded, ordinary = load_shares(number_of, rows * top, limit, lean, True), load_shares(number_of, rows * top, limit, lean, False)
    places = jnp.arange(number_of)

    def named(sizes, turn):
        used = int((sizes > 0).sum())
        fixed = max(1, used // 4)
        shifted = fixed + (places - fixed + turn * (used - fixed)) % max(1, number_of - fixed)
        return jnp.zeros((number_of,), jnp.int32).at[order[jnp.where(places < fixed, places, shifted)]].set(jnp.asarray(sizes, jnp.int32))

    sizes = jnp.where(number % 4 == 0, named(crowded, number // 4), named(ordinary, number - number // 4 - 1))
    mixed = jax.random.permutation(jax.random.fold_in(own, 3), number_of)
    source_of, taker = mixed[0:number_of // 2 * 2:2], mixed[1:number_of // 2 * 2:2]
    margin = jnp.minimum(sizes[source_of] - 1, limit - sizes[taker]) // 2
    margin = jnp.where((source_of == order[0]) | (taker == order[0]) | (sizes[taker] == 0), 0, jnp.maximum(margin, 0))
    shifted = jax.random.randint(jax.random.fold_in(own, 4), (number_of // 2,), 0, 1 << 20) % (margin + 1)
    sizes = sizes.at[source_of].add(-shifted).at[taker].add(shifted)
    labels = jnp.searchsorted(jnp.cumsum(sizes), jnp.arange(rows * top), side="right").astype(jnp.int32)
    listing = labels.reshape(top, rows).T
    listing = listing[jax.random.permutation(jax.random.fold_in(own, 1), rows)]
    turn = jax.random.randint(jax.random.fold_in(own, 2), (rows, 1), 0, top)
    return jnp.take_along_axis(listing, (jnp.arange(top)[None, :] + turn) % top, axis=1)


def load_shares(number_of, total, reach, lean, full):
    loads = [(1 << 20) // math.isqrt(grade ** lean) + 1 for grade in range(1, number_of + 1)]
    largest = reach if full else min(reach, max(-(-total // number_of), total * loads[0] // sum(loads)))
    least = 1 if total - largest >= number_of - 1 else 0
    given, surplus = [largest] + [least] * (number_of - 1), total - largest - least * (number_of - 1)
    while surplus > 0:
        free = [i for i in range(1, number_of) if given[i] < largest] or [i for i in range(1, number_of) if given[i] < reach]
        whole, left = sum([loads[i] for i in free]), surplus
        for i in free:
            addition = min(reach - given[i], max(1, left * loads[i] // whole), surplus)
            given[i] = given[i] + addition
            surplus = surplus - addition
    return np.array(given)


def noise(own_key, extent, deviation, bound, split=(), kind=jnp.bfloat16):
    factor_of = shard_levels(own_key, extent, split, -0.22, 0.18) if split else 1.0
    values = jax.random.normal(own_key, extent, jnp.float32) * deviation * factor_of
    return jnp.minimum(jnp.maximum(values, -bound), bound).astype(kind)


def setup_inputs(seed: int = 0) -> dict:
    streams_of = jax.random.split(jax.random.key(seed), 7)
    tokens = noise(streams_of[0], (TOKENS, D), 1.0, 6.0, ((0, 32),))
    grad_out = noise(streams_of[1], (TOKENS, D), 1.0, 6.0, ((0, 32),))
    expert_ids_keys = jax.random.split(jax.random.fold_in(streams_of[2], 1), TOKENS // TOK_DEV)
    expert_ids_turns = jax.random.permutation(jax.random.fold_in(streams_of[2], 3), TOKENS // TOK_DEV)
    expert_ids = jax.vmap(lambda own, number: shared_out(jax.random.fold_in(streams_of[2], 2), own, number, TOK_DEV, EXPERTS, TOP, CAP, 2))(expert_ids_keys, expert_ids_turns).reshape((TOKENS, TOP))
    gates = jnp.clip(jnp.exp(math.log(0.5) - 2.3025851 * jax.random.uniform(streams_of[3], (TOKENS, TOP), jnp.float32) ** shard_levels(streams_of[3], (TOKENS, TOP), ((0, 32),), -0.2, 0.2)), 0.05, 0.5)
    w_in = noise(streams_of[4], (EXPERTS, D, 2, H), D ** -0.5, 0.1875, ((0, 16), (3, 2)))
    w_out = noise(streams_of[5], (EXPERTS, H, D), H ** -0.5, 0.25, ((0, 16), (1, 2)))
    return {"tokens": tokens, "grad_out": grad_out, "expert_ids": expert_ids, "gates": gates, "w_in": w_in, "w_out": w_out}


def expert_pass(rows, grad_rows, weight_in, weight_out):
    model_width = rows.shape[1]
    hidden_width = weight_out.shape[0]
    flat_in = weight_in.reshape(model_width, 2 * hidden_width)
    preact = jnp.dot(rows, flat_in, preferred_element_type=jnp.float32)
    gate_part = preact[:, :hidden_width]
    up_part = preact[:, hidden_width:]
    sigmoid_gate = jax.nn.sigmoid(gate_part)
    activated = gate_part * sigmoid_gate
    hidden = (activated * up_part).astype(jnp.bfloat16)
    result = jnp.dot(hidden, weight_out, preferred_element_type=jnp.float32).astype(jnp.bfloat16)
    back_grad = jnp.dot(grad_rows, weight_out.T, preferred_element_type=jnp.float32)
    grad_gate = back_grad * up_part * (sigmoid_gate * (1.0 + gate_part * (1.0 - sigmoid_gate)))
    grad_up = back_grad * activated
    grad_pre = jnp.concatenate([grad_gate, grad_up], axis=1).astype(jnp.bfloat16)
    grad_rows_in = jnp.dot(grad_pre, flat_in.T, preferred_element_type=jnp.float32).astype(jnp.bfloat16)
    grad_weight_in = jnp.dot(rows.T, grad_pre, preferred_element_type=jnp.float32)
    grad_weight_out = jnp.dot(hidden.T, grad_rows, preferred_element_type=jnp.float32)
    return result, grad_rows_in, grad_weight_in, grad_weight_out


def reference(tokens, grad_out, expert_ids, gates, w_in, w_out):
    group_size = TOK_DEV * N_EXPERT
    row_count = group_size * TOP
    slot_count = N_EXPERT * CAP
    model_width = tokens.shape[1]
    hidden_width = w_out.shape[1]

    def expert_step(running, inputs):
        out_sum, grad_sum, gate_grad = running
        expert, weight_in, weight_out = inputs
        grad_in_sum = jnp.zeros((model_width, 2 * hidden_width), jnp.float32)
        grad_out_sum = jnp.zeros((hidden_width, model_width), jnp.float32)
        for replica in range(N_DP):
            lower = replica * group_size
            group_tokens = lax.slice_in_dim(tokens, lower, lower + group_size)
            group_grad = lax.slice_in_dim(grad_out, lower, lower + group_size)
            group_ids = lax.slice_in_dim(expert_ids, lower, lower + group_size)
            group_gates = lax.slice_in_dim(gates, lower, lower + group_size)
            flat_ids = group_ids.reshape(-1)
            positions = jnp.nonzero(flat_ids == expert, size=slot_count, fill_value=row_count)[0].astype(jnp.int32)
            valid_row = positions < row_count
            safe_rows = jnp.minimum(positions, row_count - 1).astype(jnp.int32)
            token_pos = (safe_rows // TOP).astype(jnp.int32)
            slot_k = (safe_rows % TOP).astype(jnp.int32)
            rows = jnp.where(valid_row[:, None], group_tokens[token_pos], jnp.zeros((), jnp.bfloat16))
            weight_gate = jnp.where(valid_row, group_gates[token_pos, slot_k], jnp.zeros((), jnp.float32))
            cotangent = group_grad[token_pos].astype(jnp.float32)
            grad_rows = (weight_gate[:, None] * cotangent).astype(jnp.bfloat16)
            result, grad_rows_in, grad_weight_in, grad_weight_out = expert_pass(rows, grad_rows, weight_in, weight_out)
            result_wide = result.astype(jnp.float32)
            out_sum = out_sum.at[replica, token_pos].add(weight_gate[:, None] * result_wide)
            grad_sum = grad_sum.at[replica, token_pos].add(grad_rows_in.astype(jnp.float32))
            gate_term = jnp.where(valid_row, jnp.sum(cotangent * result_wide, axis=1), jnp.zeros((), jnp.float32))
            gate_grad = gate_grad.at[replica, token_pos, slot_k].add(gate_term)
            grad_in_sum = grad_in_sum + lax.optimization_barrier(grad_weight_in.astype(jnp.bfloat16)).astype(jnp.float32)
            grad_out_sum = grad_out_sum + lax.optimization_barrier(grad_weight_out.astype(jnp.bfloat16)).astype(jnp.float32)
        stacked = grad_in_sum.reshape(model_width, 2, hidden_width)
        return (out_sum, grad_sum, gate_grad), (stacked, grad_out_sum)

    start = (jnp.zeros((N_DP, group_size, model_width), jnp.float32),
             jnp.zeros((N_DP, group_size, model_width), jnp.float32),
             jnp.zeros((N_DP, group_size, TOP), jnp.float32))
    experts_list = jnp.arange(N_EXPERT, dtype=jnp.int32)
    finals, stacked_grads = lax.scan(expert_step, start, (experts_list, w_in, w_out))
    out_sum, grad_sum, gate_grad = finals
    mixed = out_sum.reshape(TOKENS, model_width).astype(jnp.bfloat16)
    grad_tokens = grad_sum.reshape(TOKENS, model_width).astype(jnp.bfloat16)
    grad_gates = gate_grad.reshape(TOKENS, TOP)
    return mixed, grad_tokens, grad_gates, stacked_grads[0], stacked_grads[1]
```

```python
import jax
import jax.numpy as jnp
from jax import lax
from jax.sharding import PartitionSpec as P


def forward_part(rows, weight_in, weight_out):
    model_width = rows.shape[1]
    hidden_width = weight_out.shape[0]
    flat_in = weight_in.reshape(model_width, 2 * hidden_width)
    preact = jnp.dot(rows, flat_in, preferred_element_type=jnp.float32)
    gate_part = preact[:, :hidden_width]
    up_part = preact[:, hidden_width:]
    activated = gate_part * jax.nn.sigmoid(gate_part)
    hidden = (activated * up_part).astype(jnp.bfloat16)
    result = jnp.dot(hidden, weight_out, preferred_element_type=jnp.float32).astype(jnp.bfloat16)
    return (preact, hidden, result)


def backward_part(rows, preact, hidden, grad_rows, weight_in, weight_out):
    model_width = rows.shape[1]
    hidden_width = weight_out.shape[0]
    flat_in = weight_in.reshape(model_width, 2 * hidden_width)
    gate_part = preact[:, :hidden_width]
    up_part = preact[:, hidden_width:]
    sigmoid_gate = jax.nn.sigmoid(gate_part)
    activated = gate_part * sigmoid_gate
    back_grad = jnp.einsum("sd,hd->sh", grad_rows, weight_out, preferred_element_type=jnp.float32)
    grad_gate = back_grad * up_part * (sigmoid_gate * (1.0 + gate_part * (1.0 - sigmoid_gate)))
    grad_up = back_grad * activated
    grad_pre = jnp.concatenate([grad_gate, grad_up], axis=1).astype(jnp.bfloat16)
    grad_rows_in = jnp.einsum(
        "sk,dk->sd", grad_pre, flat_in, preferred_element_type=jnp.float32
    ).astype(jnp.bfloat16)
    grad_weight_in = jnp.einsum("sd,sk->dk", rows, grad_pre, preferred_element_type=jnp.float32)
    grad_weight_out = jnp.einsum("sh,sd->hd", hidden, grad_rows, preferred_element_type=jnp.float32)
    return (grad_rows_in, grad_weight_in, grad_weight_out)


def routed_plan(tokens, grad_out, expert_ids, gates, w_in, w_out):
    count_tok, model_width = tokens.shape
    per_token = expert_ids.shape[1]
    groups = lax.axis_size("expert")
    capacity = min(count_tok, 3 * count_tok * per_token // (2 * groups))
    row_count = count_tok * per_token
    flat_ids = expert_ids.reshape(-1)
    onehot = (flat_ids[:, None] == jnp.arange(groups, dtype=jnp.int32)[None, :]).astype(jnp.int32)
    order_rank = jnp.sum((jnp.cumsum(onehot, axis=0) - onehot) * onehot, axis=1)
    slot_of_row = flat_ids * capacity + order_rank
    inverse = (
        jnp.full((groups * capacity,), row_count, jnp.int32)
        .at[slot_of_row]
        .set(jnp.arange(row_count, dtype=jnp.int32))
    )
    token_of_slot = jnp.where(inverse < row_count, inverse // per_token, count_tok)
    tokens_padded = jnp.concatenate([tokens, jnp.zeros((1, model_width), jnp.bfloat16)], axis=0)
    grad_padded = jnp.concatenate([grad_out, jnp.zeros((1, model_width), jnp.bfloat16)], axis=0)
    gates_padded = jnp.concatenate([gates.reshape(-1), jnp.zeros((1,), jnp.float32)], axis=0)
    send_rows = tokens_padded[token_of_slot].reshape(groups, capacity, model_width)
    slot_gate = gates_padded[inverse]
    send_grads = (slot_gate[:, None] * grad_padded[token_of_slot].astype(jnp.float32)).astype(
        jnp.bfloat16
    )
    send_grads = send_grads.reshape(groups, capacity, model_width)
    full_in, full_out = (
        lax.all_gather(w_in, "dp", axis=3, tiled=True),
        lax.all_gather(w_out, "dp", axis=1, tiled=True),
    )
    weight_in = full_in[0]
    weight_out = full_out[0]
    hidden_width = weight_out.shape[0]
    arrived_rows = lax.all_to_all(send_rows, "expert", split_axis=0, concat_axis=0, tiled=True)
    rows = arrived_rows.reshape(groups * capacity, model_width)
    preact, hidden, result = forward_part(rows, weight_in, weight_out)
    back_out = lax.all_to_all(
        result.reshape(groups, capacity, model_width),
        "expert",
        split_axis=0,
        concat_axis=0,
        tiled=True,
    )
    arrived_grads = lax.all_to_all(send_grads, "expert", split_axis=0, concat_axis=0, tiled=True)
    grad_rows = arrived_grads.reshape(groups * capacity, model_width)
    grad_rows_in, grad_weight_in, grad_weight_out = backward_part(
        rows, preact, hidden, grad_rows, weight_in, weight_out
    )
    back_grads = lax.all_to_all(
        grad_rows_in.reshape(groups, capacity, model_width),
        "expert",
        split_axis=0,
        concat_axis=0,
        tiled=True,
    )
    out_rows = back_out.reshape(groups * capacity, model_width)[slot_of_row].reshape(
        count_tok, per_token, model_width
    )
    mixed = jnp.sum(gates[:, :, None] * out_rows.astype(jnp.float32), axis=1).astype(jnp.bfloat16)
    grad_gates = jnp.einsum("td,tkd->tk", grad_out, out_rows, preferred_element_type=jnp.float32)
    route_dx = back_grads.reshape(groups * capacity, model_width)[slot_of_row].reshape(
        count_tok, per_token, model_width
    )
    grad_tokens = jnp.sum(route_dx.astype(jnp.float32), axis=1).astype(jnp.bfloat16)
    grad_in_shard, grad_out_shard = (
        lax.psum_scatter(
            grad_weight_in.reshape(1, model_width, 2, hidden_width).astype(jnp.bfloat16),
            "dp",
            scatter_dimension=3,
            tiled=True,
        ).astype(jnp.float32),
        lax.psum_scatter(
            grad_weight_out[None].astype(jnp.bfloat16), "dp", scatter_dimension=1, tiled=True
        ).astype(jnp.float32),
    )
    return (mixed, grad_tokens, grad_gates, grad_in_shard, grad_out_shard)


def expert_math(rows, cotangent, gate, weight_in, weight_out):
    half = weight_out.shape[0]
    preact = jnp.dot(rows, weight_in, preferred_element_type=jnp.float32)
    gate_part = preact[:, :half]
    up_part = preact[:, half:]
    sig = jax.nn.sigmoid(gate_part)
    activated = gate_part * sig
    hidden = activated * up_part
    back = jnp.einsum("sd,hd->sh", cotangent, weight_out, preferred_element_type=jnp.float32)
    gate_grad = jnp.sum(hidden * back, axis=1, keepdims=True)
    gated_hidden = (gate * hidden).astype(jnp.bfloat16)
    gated_back = gate * back
    grad_gate = gated_back * up_part * (sig * (1.0 + gate_part * (1.0 - sig)))
    grad_up = gated_back * activated
    grad_pre = jnp.concatenate([grad_gate, grad_up], axis=1).astype(jnp.bfloat16)
    mixed = jnp.dot(gated_hidden, weight_out, preferred_element_type=jnp.float32)
    grad_rows = jnp.einsum("sk,dk->sd", grad_pre, weight_in, preferred_element_type=jnp.float32)
    grad_weight_in = jnp.einsum("sd,sk->dk", rows, grad_pre, preferred_element_type=jnp.float32)
    grad_weight_out = jnp.einsum(
        "sh,sd->hd", gated_hidden, cotangent, preferred_element_type=jnp.float32
    )
    return mixed, grad_rows, gate_grad, grad_weight_in, grad_weight_out


def bf16_pieces(x, count):
    pieces = []
    for _ in range(count):
        piece = x.astype(jnp.bfloat16)
        pieces.append(piece)
        x = x - piece.astype(jnp.float32)
    return pieces


def dense_plan(tokens, grad_out, expert_ids, gates, w_in, w_out):
    width = tokens.shape[1]
    groups = lax.axis_size("expert")
    mine = lax.axis_index("expert")
    experts = jnp.arange(groups, dtype=jnp.int32)
    onehot = expert_ids[:, :, None] == experts
    dense_gates = jnp.sum(jnp.where(onehot, gates[:, :, None], 0.0), axis=1)
    pieces = bf16_pieces(dense_gates, 3)
    tail = jnp.zeros((tokens.shape[0], 128 - 3 * groups), jnp.bfloat16)
    packed = jnp.concatenate([tokens, grad_out] + pieces + [tail], axis=1)
    everyone = lax.all_gather(packed, ("dp", "expert"), axis=0, tiled=True)
    rows = everyone[:, :width]
    cotangent = everyone[:, width : 2 * width]
    three = everyone[:, 2 * width : 2 * width + 3 * groups].astype(jnp.float32)
    all_gates = three[:, :groups] + three[:, groups : 2 * groups] + three[:, 2 * groups :]
    gate = jnp.sum(jnp.where(experts == mine, all_gates, 0.0), axis=1, keepdims=True)
    half = w_out.shape[1]
    mixed, grad_rows, gate_grad, grad_weight_in, grad_weight_out = expert_math(
        rows, cotangent, gate, w_in.reshape(width, 2 * half), w_out[0]
    )
    spread = jnp.where(experts == mine, gate_grad, 0.0)
    tail = jnp.zeros((rows.shape[0], 128 - 2 * groups), jnp.bfloat16)
    partial = jnp.concatenate(
        [mixed.astype(jnp.bfloat16), grad_rows.astype(jnp.bfloat16)]
        + bf16_pieces(spread, 2)
        + [tail],
        axis=1,
    )
    total = lax.psum_scatter(partial, ("dp", "expert"), scatter_dimension=0, tiled=True)
    two = total[:, 2 * width : 2 * width + 2 * groups].astype(jnp.float32)
    by_expert = two[:, :groups] + two[:, groups:]
    grad_gates = jnp.sum(jnp.where(onehot, by_expert[:, None, :], 0.0), axis=2)
    return (
        total[:, :width],
        total[:, width : 2 * width],
        grad_gates,
        grad_weight_in.reshape(w_in.shape),
        grad_weight_out[None],
    )


def per_device(tokens, grad_out, expert_ids, gates, w_in, w_out):
    if lax.axis_size("expert") > 4 * expert_ids.shape[1]:
        return routed_plan(tokens, grad_out, expert_ids, gates, w_in, w_out)
    return dense_plan(tokens, grad_out, expert_ids, gates, w_in, w_out)


def solution(mesh):
    in_specs = (
        P(("dp", "expert"), None),
        P(("dp", "expert"), None),
        P(("dp", "expert"), None),
        P(("dp", "expert"), None),
        P("expert", None, None, "dp"),
        P("expert", "dp", None),
    )
    out_specs = (
        P(("dp", "expert"), None),
        P(("dp", "expert"), None),
        P(("dp", "expert"), None),
        P("expert", None, None, "dp"),
        P("expert", "dp", None),
    )
    return jax.shard_map(
        per_device, mesh=mesh, in_specs=in_specs, out_specs=out_specs, check_vma=False
    )
```

```python
import functools

import jax
import jax.numpy as jnp
from jax import lax
from jax.experimental import pallas as pl
from jax.experimental.pallas import tpu as pltpu
from jax.sharding import PartitionSpec as P


def forward_part(rows, weight_in, weight_out):
    model_width = rows.shape[1]
    hidden_width = weight_out.shape[0]
    flat_in = weight_in.reshape(model_width, 2 * hidden_width)
    preact = jnp.dot(rows, flat_in, preferred_element_type=jnp.float32)
    gate_part = preact[:, :hidden_width]
    up_part = preact[:, hidden_width:]
    activated = gate_part * jax.nn.sigmoid(gate_part)
    hidden = (activated * up_part).astype(jnp.bfloat16)
    result = jnp.dot(hidden, weight_out, preferred_element_type=jnp.float32).astype(jnp.bfloat16)
    return (preact, hidden, result)


def backward_part(rows, preact, hidden, grad_rows, weight_in, weight_out):
    model_width = rows.shape[1]
    hidden_width = weight_out.shape[0]
    flat_in = weight_in.reshape(model_width, 2 * hidden_width)
    gate_part = preact[:, :hidden_width]
    up_part = preact[:, hidden_width:]
    sigmoid_gate = jax.nn.sigmoid(gate_part)
    activated = gate_part * sigmoid_gate
    back_grad = jnp.einsum("sd,hd->sh", grad_rows, weight_out, preferred_element_type=jnp.float32)
    grad_gate = back_grad * up_part * (sigmoid_gate * (1.0 + gate_part * (1.0 - sigmoid_gate)))
    grad_up = back_grad * activated
    grad_pre = jnp.concatenate([grad_gate, grad_up], axis=1).astype(jnp.bfloat16)
    grad_rows_in = jnp.einsum(
        "sk,dk->sd", grad_pre, flat_in, preferred_element_type=jnp.float32
    ).astype(jnp.bfloat16)
    grad_weight_in = jnp.einsum("sd,sk->dk", rows, grad_pre, preferred_element_type=jnp.float32)
    grad_weight_out = jnp.einsum("sh,sd->hd", hidden, grad_rows, preferred_element_type=jnp.float32)
    return (grad_rows_in, grad_weight_in, grad_weight_out)


def routed_plan(tokens, grad_out, expert_ids, gates, w_in, w_out):
    count_tok, model_width = tokens.shape
    per_token = expert_ids.shape[1]
    groups = lax.axis_size("expert")
    capacity = min(count_tok, 3 * count_tok * per_token // (2 * groups))
    row_count = count_tok * per_token
    flat_ids = expert_ids.reshape(-1)
    onehot = (flat_ids[:, None] == jnp.arange(groups, dtype=jnp.int32)[None, :]).astype(jnp.int32)
    order_rank = jnp.sum((jnp.cumsum(onehot, axis=0) - onehot) * onehot, axis=1)
    slot_of_row = flat_ids * capacity + order_rank
    inverse = (
        jnp.full((groups * capacity,), row_count, jnp.int32)
        .at[slot_of_row]
        .set(jnp.arange(row_count, dtype=jnp.int32))
    )
    token_of_slot = jnp.where(inverse < row_count, inverse // per_token, count_tok)
    tokens_padded = jnp.concatenate([tokens, jnp.zeros((1, model_width), jnp.bfloat16)], axis=0)
    grad_padded = jnp.concatenate([grad_out, jnp.zeros((1, model_width), jnp.bfloat16)], axis=0)
    gates_padded = jnp.concatenate([gates.reshape(-1), jnp.zeros((1,), jnp.float32)], axis=0)
    send_rows = tokens_padded[token_of_slot].reshape(groups, capacity, model_width)
    slot_gate = gates_padded[inverse]
    send_grads = (slot_gate[:, None] * grad_padded[token_of_slot].astype(jnp.float32)).astype(
        jnp.bfloat16
    )
    send_grads = send_grads.reshape(groups, capacity, model_width)
    full_in, full_out = (
        lax.all_gather(w_in, "dp", axis=3, tiled=True),
        lax.all_gather(w_out, "dp", axis=1, tiled=True),
    )
    weight_in = full_in[0]
    weight_out = full_out[0]
    hidden_width = weight_out.shape[0]
    arrived_rows = lax.all_to_all(send_rows, "expert", split_axis=0, concat_axis=0, tiled=True)
    rows = arrived_rows.reshape(groups * capacity, model_width)
    preact, hidden, result = forward_part(rows, weight_in, weight_out)
    back_out = lax.all_to_all(
        result.reshape(groups, capacity, model_width),
        "expert",
        split_axis=0,
        concat_axis=0,
        tiled=True,
    )
    arrived_grads = lax.all_to_all(send_grads, "expert", split_axis=0, concat_axis=0, tiled=True)
    grad_rows = arrived_grads.reshape(groups * capacity, model_width)
    grad_rows_in, grad_weight_in, grad_weight_out = backward_part(
        rows, preact, hidden, grad_rows, weight_in, weight_out
    )
    back_grads = lax.all_to_all(
        grad_rows_in.reshape(groups, capacity, model_width),
        "expert",
        split_axis=0,
        concat_axis=0,
        tiled=True,
    )
    out_rows = back_out.reshape(groups * capacity, model_width)[slot_of_row].reshape(
        count_tok, per_token, model_width
    )
    mixed = jnp.sum(gates[:, :, None] * out_rows.astype(jnp.float32), axis=1).astype(jnp.bfloat16)
    grad_gates = jnp.einsum("td,tkd->tk", grad_out, out_rows, preferred_element_type=jnp.float32)
    route_dx = back_grads.reshape(groups * capacity, model_width)[slot_of_row].reshape(
        count_tok, per_token, model_width
    )
    grad_tokens = jnp.sum(route_dx.astype(jnp.float32), axis=1).astype(jnp.bfloat16)
    grad_in_shard, grad_out_shard = (
        lax.psum_scatter(
            grad_weight_in.reshape(1, model_width, 2, hidden_width).astype(jnp.bfloat16),
            "dp",
            scatter_dimension=3,
            tiled=True,
        ).astype(jnp.float32),
        lax.psum_scatter(
            grad_weight_out[None].astype(jnp.bfloat16), "dp", scatter_dimension=1, tiled=True
        ).astype(jnp.float32),
    )
    return (mixed, grad_tokens, grad_gates, grad_in_shard, grad_out_shard)


MESH = pl.DeviceIdType.MESH
GATE_COLS = 128


def dot_nt(a, b):
    return lax.dot_general(a, b, (((1,), (1,)), ((), ())), preferred_element_type=jnp.float32)


def dot_tn(a, b):
    return lax.dot_general(a, b, (((0,), (0,)), ((), ())), preferred_element_type=jnp.float32)


def moe_kernel(
    groups, tokens_ref, cot_ref, ids_ref, gates_ref, w_in_ref, w_out_ref,
    mixed_ref, grad_tok_ref, grad_gates_ref, grad_in_ref, grad_out_ref,
    tok_all, cot_all, part_mixed, part_grad, recv_mixed, recv_grad,
    rows_buf, cot_buf, hidden_buf, pre_buf,
    gather_send, gather_recv, scatter_send, scatter_recv,
):
    count, width = tokens_ref.shape
    per_token = ids_ref.shape[1]
    half = w_out_ref.shape[0]
    chunk = 8 * count
    x = lax.axis_index("dp")
    e = lax.axis_index("expert")
    z, y, c = e // 4, (e // 2) % 2, e % 2

    def place(px, pz, py, pc):
        return (px, pz * 4 + py * 2 + pc)

    to_z = {
        1: place(x, z + 1 - 2 * (z % 2), y, c),
        2: place(x, (z + 2) % 4, y, c),
        3: place(x, 3 - z, y, c),
    }
    to_x = place(1 - x, z, y, c)
    to_y = place(x, z, 1 - y, c)
    to_core = place(x, z, y, 1 - c)

    partners = [to_z[1], to_z[2], to_z[3], to_x, to_y, to_core]
    barrier = pltpu.get_barrier_semaphore()
    for partner in partners:
        pl.semaphore_signal(barrier, inc=1, device_id=partner, device_id_type=MESH)

    col = lax.broadcasted_iota(jnp.int32, (count, GATE_COLS), 1)
    ids = ids_ref[...]
    gates = gates_ref[...]
    dense = jnp.zeros((count, GATE_COLS), jnp.float32)
    for k in range(per_token):
        dense = dense + jnp.where(ids[:, k : k + 1] == col % groups, gates[:, k : k + 1], 0.0)
    high = dense.astype(jnp.bfloat16).astype(jnp.float32)
    middle = (dense - high).astype(jnp.bfloat16).astype(jnp.float32)
    low = dense - high - middle
    pieces = jnp.where(
        col < groups,
        high,
        jnp.where(col < 2 * groups, middle, jnp.where(col < 3 * groups, low, 0.0)),
    )
    tok_all[0, :, :width] = tokens_ref[...]
    tok_all[0, :, width:] = pieces.astype(jnp.bfloat16)
    cot_all[0] = cot_ref[...]
    pl.semaphore_wait(barrier, len(partners))

    gathered = (tok_all, cot_all)
    sent = []

    def push(h, src, dst, device):
        copy = pltpu.make_async_remote_copy(
            src_ref=gathered[h].at[src],
            dst_ref=gathered[h].at[dst],
            send_sem=gather_send.at[h, dst],
            recv_sem=gather_recv.at[h, dst],
            device_id=device,
            device_id_type=MESH,
        )
        copy.start()
        sent.append(copy)

    def arrived(h, slot):
        pltpu.make_async_remote_copy(
            src_ref=gathered[h].at[slot],
            dst_ref=gathered[h].at[slot],
            send_sem=gather_send.at[h, slot],
            recv_sem=gather_recv.at[h, slot],
            device_id=to_core,
            device_id_type=MESH,
        ).wait_recv()

    first = (to_x, to_y)
    second = (to_y, to_x)
    first_q = (2, 1)
    second_q = (1, 2)
    order = (0, 1, 3, 2)
    for dz in (1, 3, 2):
        for h in (0, 1):
            push(h, 0, dz, to_z[dz])
    for dz in order:
        for h in (0, 1):
            if dz:
                arrived(h, dz)
            push(h, dz, 8 * first_q[h] + dz, first[h])
            push(h, dz, 8 * second_q[h] + dz, second[h])
            push(h, dz, 4 + dz, to_core)
    for dz in order:
        for h in (0, 1):
            slot = 8 * first_q[h] + dz
            arrived(h, slot)
            push(h, slot, 24 + dz, second[h])
            push(h, slot, slot + 4, to_core)

    partial = (part_mixed, part_grad)
    landing = (recv_mixed, recv_grad)

    def give(h, src, dst, device, number=1):
        copy = pltpu.make_async_remote_copy(
            src_ref=partial[h].at[pl.ds(src, number)],
            dst_ref=landing[h].at[pl.ds(dst, number)],
            send_sem=scatter_send.at[h, dst],
            recv_sem=scatter_recv.at[h, dst],
            device_id=device,
            device_id_type=MESH,
        )
        copy.start()
        sent.append(copy)

    def took(h, dst, number=1):
        pltpu.make_async_remote_copy(
            src_ref=partial[h].at[pl.ds(0, number)],
            dst_ref=landing[h].at[pl.ds(dst, number)],
            send_sem=scatter_send.at[h, dst],
            recv_sem=scatter_recv.at[h, dst],
            device_id=to_core,
            device_id_type=MESH,
        ).wait_recv()

    def add(h, slot, dst):
        partial[h][slot] = (
            partial[h][slot].astype(jnp.float32) + landing[h][dst].astype(jnp.float32)
        ).astype(jnp.bfloat16)

    wide_col = lax.broadcasted_iota(jnp.int32, (chunk, GATE_COLS), 1)

    def compute(q):
        block = pl.ds(8 * q, 8)
        here = pl.ds(chunk * q, chunk)
        packed = tok_all[block].astype(jnp.float32).reshape(chunk, width + GATE_COLS)
        rows = packed[:, :width].astype(jnp.bfloat16)
        cot = cot_all[block].astype(jnp.float32).reshape(chunk, width).astype(jnp.bfloat16)
        own = jnp.logical_and(wide_col % groups == e, wide_col < 3 * groups)
        gate = jnp.sum(jnp.where(own, packed[:, width:], 0.0), axis=1, keepdims=True)
        rows_buf[here, :] = rows
        cot_buf[here, :] = cot
        preact = jnp.dot(rows, w_in_ref[...], preferred_element_type=jnp.float32)
        gate_part = preact[:, :half]
        up_part = preact[:, half:]
        sig = jax.nn.sigmoid(gate_part)
        activated = gate_part * sig
        hidden = activated * up_part
        back = dot_nt(cot, w_out_ref[...])
        gate_grad = jnp.sum(hidden * back, axis=1, keepdims=True)
        gated_hidden = (gate * hidden).astype(jnp.bfloat16)
        gated_back = gate * back
        grad_gate = gated_back * up_part * (sig * (1.0 + gate_part * (1.0 - sig)))
        grad_up = gated_back * activated
        grad_pre = jnp.concatenate([grad_gate, grad_up], axis=1).astype(jnp.bfloat16)
        hidden_buf[here, :] = gated_hidden
        pre_buf[here, :] = grad_pre
        mixed = jnp.dot(gated_hidden, w_out_ref[...], preferred_element_type=jnp.float32)
        part_mixed[block, :, :width] = mixed.reshape(8, count, width).astype(jnp.bfloat16)
        high = gate_grad.astype(jnp.bfloat16).astype(jnp.float32)
        spread = jnp.where(
            wide_col == e, high, jnp.where(wide_col == groups + e, gate_grad - high, 0.0)
        )
        part_mixed[block, :, width:] = spread.reshape(8, count, GATE_COLS).astype(jnp.bfloat16)
        grad_rows = dot_nt(grad_pre, w_in_ref[...])
        part_grad[block] = grad_rows.reshape(8, count, width).astype(jnp.bfloat16)
        for h in (0, 1):
            give(h, 8 * q + 4, 4 * q, to_core, 4)

    def fold_core(q):
        for h in (0, 1):
            took(h, 4 * q, 4)
            for dz in range(4):
                add(h, 8 * q + dz, 4 * q + dz)

    def wait_core(q):
        for dz in order:
            for h in (0, 1):
                arrived(h, 8 * q + 4 + dz)

    wait_core(0)
    compute(0)
    for dz in order:
        for h in (0, 1):
            slot = 8 * second_q[h] + dz
            arrived(h, slot)
            push(h, slot, slot + 4, to_core)
    wait_core(2)
    compute(2)
    wait_core(1)
    compute(1)
    for dz in order:
        for h in (0, 1):
            arrived(h, 24 + dz)
            push(h, 24 + dz, 28 + dz, to_core)
    fold_core(0)
    one = (to_y, to_x)
    two = (to_x, to_y)
    back_order = (2, 3, 1, 0)
    fold_core(2)
    fold_core(1)
    wait_core(3)
    compute(3)
    fold_core(3)
    for dz in back_order:
        for h in (0, 1):
            give(h, 24 + dz, 20 + dz, one[h])
    for dz in back_order:
        for h in (0, 1):
            give(h, 8 * (1, 2)[h] + dz, 16 + dz, one[h])
    grad_out_ref[...] = dot_tn(hidden_buf[...], cot_buf[...])
    for dz in back_order:
        for h in (0, 1):
            took(h, 20 + dz)
            slot = 8 * (2, 1)[h] + dz
            add(h, slot, 20 + dz)
            give(h, slot, 24 + dz, two[h])
    grad_in_ref[...] = dot_tn(rows_buf[...], pre_buf[...])
    for dz in back_order:
        for h in (0, 1):
            took(h, 16 + dz)
            add(h, dz, 16 + dz)
            took(h, 24 + dz)
            add(h, dz, 24 + dz)
            if dz:
                give(h, dz, 28 + dz, to_z[dz])
    totals = []
    for h in (0, 1):
        total = partial[h][0].astype(jnp.float32)
        for dz in (1, 3, 2):
            took(h, 28 + dz)
            total = total + landing[h][28 + dz].astype(jnp.float32)
        totals.append(total)
    mixed_ref[...] = totals[0][:, :width].astype(jnp.bfloat16)
    grad_tok_ref[...] = totals[1].astype(jnp.bfloat16)
    by_expert = totals[0][:, width:]
    columns = []
    for k in range(per_token):
        chosen = jnp.logical_and(col % groups == ids[:, k : k + 1], col < 2 * groups)
        columns.append(jnp.sum(jnp.where(chosen, by_expert, 0.0), axis=1, keepdims=True))
    grad_gates_ref[...] = jnp.concatenate(columns, axis=1)
    for copy in sent:
        copy.wait_send()


def dense_plan(tokens, grad_out, expert_ids, gates, w_in, w_out):
    count, width = tokens.shape
    groups = lax.axis_size("expert")
    half = w_out.shape[1]
    devices = 2 * groups
    vmem = pl.BlockSpec(memory_space=pltpu.VMEM)
    total_rows = devices * count
    wide = width + GATE_COLS
    outs = pl.pallas_call(
        functools.partial(moe_kernel, groups),
        out_shape=(
            jax.ShapeDtypeStruct((count, width), jnp.bfloat16),
            jax.ShapeDtypeStruct((count, width), jnp.bfloat16),
            jax.ShapeDtypeStruct(gates.shape, jnp.float32),
            jax.ShapeDtypeStruct((width, 2 * half), jnp.float32),
            jax.ShapeDtypeStruct((half, width), jnp.float32),
        ),
        in_specs=[vmem] * 6,
        out_specs=[vmem] * 5,
        scratch_shapes=[
            pltpu.VMEM((devices, count, wide), jnp.bfloat16),
            pltpu.VMEM((devices, count, width), jnp.bfloat16),
            pltpu.VMEM((devices, count, wide), jnp.bfloat16),
            pltpu.VMEM((devices, count, width), jnp.bfloat16),
            pltpu.VMEM((devices, count, wide), jnp.bfloat16),
            pltpu.VMEM((devices, count, width), jnp.bfloat16),
            pltpu.VMEM((total_rows, width), jnp.bfloat16),
            pltpu.VMEM((total_rows, width), jnp.bfloat16),
            pltpu.VMEM((total_rows, half), jnp.bfloat16),
            pltpu.VMEM((total_rows, 2 * half), jnp.bfloat16),
            pltpu.SemaphoreType.DMA((2, devices)),
            pltpu.SemaphoreType.DMA((2, devices)),
            pltpu.SemaphoreType.DMA((2, devices)),
            pltpu.SemaphoreType.DMA((2, devices)),
        ],
        compiler_params=pltpu.CompilerParams(
            collective_id=0, has_side_effects=True, vmem_limit_bytes=52 * 1024 * 1024
        ),
        cost_estimate=pl.CostEstimate(
            flops=18 * total_rows * width * half,
            bytes_accessed=12 * width * half + 6 * width * half,
            transcendentals=total_rows * half,
        ),
    )(tokens, grad_out, expert_ids, gates, w_in.reshape(width, 2 * half), w_out[0])
    mixed, grad_tokens, grad_gates, grad_in, grad_out_w = outs
    return (mixed, grad_tokens, grad_gates, grad_in.reshape(w_in.shape), grad_out_w[None])


def per_device(tokens, grad_out, expert_ids, gates, w_in, w_out):
    if lax.axis_size("expert") == 16 and lax.axis_size("dp") == 2:
        return dense_plan(tokens, grad_out, expert_ids, gates, w_in, w_out)
    return routed_plan(tokens, grad_out, expert_ids, gates, w_in, w_out)


def solution(mesh):
    in_specs = (
        P(("dp", "expert"), None),
        P(("dp", "expert"), None),
        P(("dp", "expert"), None),
        P(("dp", "expert"), None),
        P("expert", None, None, "dp"),
        P("expert", "dp", None),
    )
    out_specs = (
        P(("dp", "expert"), None),
        P(("dp", "expert"), None),
        P(("dp", "expert"), None),
        P("expert", None, None, "dp"),
        P("expert", "dp", None),
    )
    return jax.shard_map(
        per_device, mesh=mesh, in_specs=in_specs, out_specs=out_specs, check_vma=False
    )
```

```python
import functools

import jax
import jax.numpy as jnp
from jax import lax
from jax.experimental import pallas as pl
from jax.experimental.pallas import tpu as pltpu
from jax.sharding import PartitionSpec as P


def forward_part(rows, weight_in, weight_out):
    model_width = rows.shape[1]
    hidden_width = weight_out.shape[0]
    flat_in = weight_in.reshape(model_width, 2 * hidden_width)
    preact = jnp.dot(rows, flat_in, preferred_element_type=jnp.float32)
    gate_part = preact[:, :hidden_width]
    up_part = preact[:, hidden_width:]
    activated = gate_part * jax.nn.sigmoid(gate_part)
    hidden = (activated * up_part).astype(jnp.bfloat16)
    result = jnp.dot(hidden, weight_out, preferred_element_type=jnp.float32).astype(jnp.bfloat16)
    return (preact, hidden, result)


def backward_part(rows, preact, hidden, grad_rows, weight_in, weight_out):
    model_width = rows.shape[1]
    hidden_width = weight_out.shape[0]
    flat_in = weight_in.reshape(model_width, 2 * hidden_width)
    gate_part = preact[:, :hidden_width]
    up_part = preact[:, hidden_width:]
    sigmoid_gate = jax.nn.sigmoid(gate_part)
    activated = gate_part * sigmoid_gate
    back_grad = jnp.einsum("sd,hd->sh", grad_rows, weight_out, preferred_element_type=jnp.float32)
    grad_gate = back_grad * up_part * (sigmoid_gate * (1.0 + gate_part * (1.0 - sigmoid_gate)))
    grad_up = back_grad * activated
    grad_pre = jnp.concatenate([grad_gate, grad_up], axis=1).astype(jnp.bfloat16)
    grad_rows_in = jnp.einsum(
        "sk,dk->sd", grad_pre, flat_in, preferred_element_type=jnp.float32
    ).astype(jnp.bfloat16)
    grad_weight_in = jnp.einsum("sd,sk->dk", rows, grad_pre, preferred_element_type=jnp.float32)
    grad_weight_out = jnp.einsum("sh,sd->hd", hidden, grad_rows, preferred_element_type=jnp.float32)
    return (grad_rows_in, grad_weight_in, grad_weight_out)


def routed_plan(tokens, grad_out, expert_ids, gates, w_in, w_out):
    count_tok, model_width = tokens.shape
    per_token = expert_ids.shape[1]
    groups = lax.axis_size("expert")
    capacity = min(count_tok, 3 * count_tok * per_token // (2 * groups))
    row_count = count_tok * per_token
    flat_ids = expert_ids.reshape(-1)
    onehot = (flat_ids[:, None] == jnp.arange(groups, dtype=jnp.int32)[None, :]).astype(jnp.int32)
    order_rank = jnp.sum((jnp.cumsum(onehot, axis=0) - onehot) * onehot, axis=1)
    slot_of_row = flat_ids * capacity + order_rank
    inverse = (
        jnp.full((groups * capacity,), row_count, jnp.int32)
        .at[slot_of_row]
        .set(jnp.arange(row_count, dtype=jnp.int32))
    )
    token_of_slot = jnp.where(inverse < row_count, inverse // per_token, count_tok)
    tokens_padded = jnp.concatenate([tokens, jnp.zeros((1, model_width), jnp.bfloat16)], axis=0)
    grad_padded = jnp.concatenate([grad_out, jnp.zeros((1, model_width), jnp.bfloat16)], axis=0)
    gates_padded = jnp.concatenate([gates.reshape(-1), jnp.zeros((1,), jnp.float32)], axis=0)
    send_rows = tokens_padded[token_of_slot].reshape(groups, capacity, model_width)
    slot_gate = gates_padded[inverse]
    send_grads = (slot_gate[:, None] * grad_padded[token_of_slot].astype(jnp.float32)).astype(
        jnp.bfloat16
    )
    send_grads = send_grads.reshape(groups, capacity, model_width)
    full_in, full_out = (
        lax.all_gather(w_in, "dp", axis=3, tiled=True),
        lax.all_gather(w_out, "dp", axis=1, tiled=True),
    )
    weight_in = full_in[0]
    weight_out = full_out[0]
    hidden_width = weight_out.shape[0]
    arrived_rows = lax.all_to_all(send_rows, "expert", split_axis=0, concat_axis=0, tiled=True)
    rows = arrived_rows.reshape(groups * capacity, model_width)
    preact, hidden, result = forward_part(rows, weight_in, weight_out)
    back_out = lax.all_to_all(
        result.reshape(groups, capacity, model_width),
        "expert",
        split_axis=0,
        concat_axis=0,
        tiled=True,
    )
    arrived_grads = lax.all_to_all(send_grads, "expert", split_axis=0, concat_axis=0, tiled=True)
    grad_rows = arrived_grads.reshape(groups * capacity, model_width)
    grad_rows_in, grad_weight_in, grad_weight_out = backward_part(
        rows, preact, hidden, grad_rows, weight_in, weight_out
    )
    back_grads = lax.all_to_all(
        grad_rows_in.reshape(groups, capacity, model_width),
        "expert",
        split_axis=0,
        concat_axis=0,
        tiled=True,
    )
    out_rows = back_out.reshape(groups * capacity, model_width)[slot_of_row].reshape(
        count_tok, per_token, model_width
    )
    mixed = jnp.sum(gates[:, :, None] * out_rows.astype(jnp.float32), axis=1).astype(jnp.bfloat16)
    grad_gates = jnp.einsum("td,tkd->tk", grad_out, out_rows, preferred_element_type=jnp.float32)
    route_dx = back_grads.reshape(groups * capacity, model_width)[slot_of_row].reshape(
        count_tok, per_token, model_width
    )
    grad_tokens = jnp.sum(route_dx.astype(jnp.float32), axis=1).astype(jnp.bfloat16)
    grad_in_shard, grad_out_shard = (
        lax.psum_scatter(
            grad_weight_in.reshape(1, model_width, 2, hidden_width).astype(jnp.bfloat16),
            "dp",
            scatter_dimension=3,
            tiled=True,
        ).astype(jnp.float32),
        lax.psum_scatter(
            grad_weight_out[None].astype(jnp.bfloat16), "dp", scatter_dimension=1, tiled=True
        ).astype(jnp.float32),
    )
    return (mixed, grad_tokens, grad_gates, grad_in_shard, grad_out_shard)


MESH = pl.DeviceIdType.MESH
GATE_COLS = 128


def dot_nt(a, b):
    return lax.dot_general(a, b, (((1,), (1,)), ((), ())), preferred_element_type=jnp.float32)


def dot_tn(a, b):
    return lax.dot_general(a, b, (((0,), (0,)), ((), ())), preferred_element_type=jnp.float32)


def moe_kernel(
    groups, tokens_ref, cot_ref, ids_ref, gates_ref, w_in_hbm, w_out_hbm,
    mixed_ref, grad_tok_ref, grad_gates_ref, grad_in_hbm, grad_out_hbm,
    tok_all, cot_all, part_mixed, part_grad, recv_mixed, recv_grad,
    rows_buf, cot_buf, hidden_buf, pre_buf, w_in_ref, w_out_ref, grad_in_ref, grad_out_ref,
    gather_send, gather_recv, scatter_send, scatter_recv, local_sem,
):
    count, width = tokens_ref.shape
    per_token = ids_ref.shape[0]
    half = w_out_ref.shape[0]
    batches, blocks, batch = tok_all.shape[:3]
    chunk = blocks * batch
    x = lax.axis_index("dp")
    e = lax.axis_index("expert")
    z, y, c = e // 4, (e // 2) % 2, e % 2

    def place(px, pz, py, pc):
        return (px, pz * 4 + py * 2 + pc)

    to_z = {
        1: place(x, z + 1 - 2 * (z % 2), y, c),
        2: place(x, (z + 2) % 4, y, c),
        3: place(x, 3 - z, y, c),
    }
    to_x = place(1 - x, z, y, c)
    to_y = place(x, z, 1 - y, c)
    to_core = place(x, z, y, 1 - c)

    partners = [to_z[1], to_z[2], to_z[3], to_x, to_y, to_core]
    barrier = pltpu.get_barrier_semaphore()
    for partner in partners:
        pl.semaphore_signal(barrier, inc=1, device_id=partner, device_id_type=MESH)
    load_in = pltpu.make_async_copy(w_in_hbm, w_in_ref, local_sem.at[0])
    load_out = pltpu.make_async_copy(w_out_hbm, w_out_ref, local_sem.at[1])
    load_in.start()
    load_out.start()

    col = lax.broadcasted_iota(jnp.int32, (count, GATE_COLS), 1)
    col_expert = (col % groups).astype(jnp.float32)
    diagonal = lax.broadcasted_iota(jnp.int32, (count, count), 0) == lax.broadcasted_iota(
        jnp.int32, (count, count), 1
    )
    ids_t = ids_ref[...].astype(jnp.float32)
    gates_t = gates_ref[...]

    def column(table, k):
        return jnp.sum(jnp.where(diagonal, table[k : k + 1, :], 0.0), axis=1, keepdims=True)

    ids = [column(ids_t, k) for k in range(per_token)]
    dense = jnp.zeros((count, GATE_COLS), jnp.float32)
    for k in range(per_token):
        dense = dense + jnp.where(ids[k] == col_expert, column(gates_t, k), 0.0)
    high = dense.astype(jnp.bfloat16).astype(jnp.float32)
    middle = (dense - high).astype(jnp.bfloat16).astype(jnp.float32)
    low = dense - high - middle
    pieces = jnp.where(
        col < groups,
        high,
        jnp.where(col < 2 * groups, middle, jnp.where(col < 3 * groups, low, 0.0)),
    )
    own_tokens = tokens_ref[...].astype(jnp.float32)
    own_cot = cot_ref[...].astype(jnp.float32)
    for g in range(batches):
        part = slice(g * batch, (g + 1) * batch)
        tok_all[g, 0, :, :width] = own_tokens[part].astype(jnp.bfloat16)
        tok_all[g, 0, :, width:] = pieces[part].astype(jnp.bfloat16)
        cot_all[g, 0] = own_cot[part].astype(jnp.bfloat16)
    pl.semaphore_wait(barrier, len(partners))

    gathered = (tok_all, cot_all)
    partial = (part_mixed, part_grad)
    landing = (recv_mixed, recv_grad)
    sent = []

    def copy_of(source, target, sems, g, h, src, dst, device, number):
        return pltpu.make_async_remote_copy(
            src_ref=source[h].at[g, pl.ds(src, number)],
            dst_ref=target[h].at[g, pl.ds(dst, number)],
            send_sem=sems[0].at[g, h, dst],
            recv_sem=sems[1].at[g, h, dst],
            device_id=device,
            device_id_type=MESH,
        )

    gather_sems = (gather_send, gather_recv)
    scatter_sems = (scatter_send, scatter_recv)

    def push(g, h, src, dst, device, number=4):
        copy = copy_of(gathered, gathered, gather_sems, g, h, src, dst, device, number)
        copy.start()
        sent.append(copy)

    def arrived(g, h, slot, number=4):
        copy_of(gathered, gathered, gather_sems, g, h, slot, slot, to_core, number).wait_recv()

    def give(g, h, src, dst, device, number=4):
        copy = copy_of(partial, landing, scatter_sems, g, h, src, dst, device, number)
        copy.start()
        sent.append(copy)

    def took(g, h, dst, number=4):
        copy_of(partial, landing, scatter_sems, g, h, 0, dst, to_core, number).wait_recv()

    def add(g, h, slot, dst, number=4):
        here = pl.ds(slot, number)
        partial[h][g, here] = (
            partial[h][g, here].astype(jnp.float32)
            + landing[h][g, pl.ds(dst, number)].astype(jnp.float32)
        ).astype(jnp.bfloat16)

    first = (to_x, to_y)
    second = (to_y, to_x)
    first_slot = (8, 4)
    second_slot = (4, 8)

    def gather_z(g):
        for dz in (1, 3, 2):
            for h in (0, 1):
                push(g, h, 0, dz, to_z[dz], 1)

    def gather_plane(g):
        for h in (0, 1):
            for dz in (1, 3, 2):
                arrived(g, h, dz, 1)
            push(g, h, 0, first_slot[h], first[h])
            push(g, h, 0, second_slot[h], second[h])
            push(g, h, 0, 16, to_core)

    def gather_far(g):
        for h in (0, 1):
            slot = first_slot[h]
            arrived(g, h, slot)
            push(g, h, slot, 12, second[h])
            push(g, h, slot, 16 + slot, to_core)

    def gather_core(g):
        for h in (0, 1):
            slot = second_slot[h]
            arrived(g, h, slot)
            push(g, h, slot, 16 + slot, to_core)
        for h in (0, 1):
            arrived(g, h, 12)
            push(g, h, 12, 28, to_core)

    def gather_end(g):
        for slot in (16, 20, 24, 28):
            for h in (0, 1):
                arrived(g, h, slot)

    wide_col = lax.broadcasted_iota(jnp.int32, (chunk, GATE_COLS), 1)

    def compute(g):
        here = pl.ds(chunk * g, chunk)
        packed = tok_all[g].astype(jnp.float32).reshape(chunk, width + GATE_COLS)
        rows = packed[:, :width].astype(jnp.bfloat16)
        cot = cot_all[g].astype(jnp.float32).reshape(chunk, width).astype(jnp.bfloat16)
        own = jnp.logical_and(wide_col % groups == e, wide_col < 3 * groups)
        gate = jnp.sum(jnp.where(own, packed[:, width:], 0.0), axis=1, keepdims=True)
        rows_buf[here, :] = rows
        cot_buf[here, :] = cot
        preact = jnp.dot(rows, w_in_ref[...], preferred_element_type=jnp.float32)
        gate_part = preact[:, :half]
        up_part = preact[:, half:]
        sig = jax.nn.sigmoid(gate_part)
        activated = gate_part * sig
        hidden = activated * up_part
        back = dot_nt(cot, w_out_ref[...])
        gate_grad = jnp.sum(hidden * back, axis=1, keepdims=True)
        gated_hidden = (gate * hidden).astype(jnp.bfloat16)
        gated_back = gate * back
        grad_gate = gated_back * up_part * (sig * (1.0 + gate_part * (1.0 - sig)))
        grad_up = gated_back * activated
        grad_pre = jnp.concatenate([grad_gate, grad_up], axis=1).astype(jnp.bfloat16)
        hidden_buf[here, :] = gated_hidden
        pre_buf[here, :] = grad_pre
        mixed = jnp.dot(gated_hidden, w_out_ref[...], preferred_element_type=jnp.float32)
        part_mixed[g, :, :, :width] = mixed.reshape(blocks, batch, width).astype(jnp.bfloat16)
        high = gate_grad.astype(jnp.bfloat16).astype(jnp.float32)
        spread = jnp.where(
            wide_col == e, high, jnp.where(wide_col == groups + e, gate_grad - high, 0.0)
        )
        part_mixed[g, :, :, width:] = spread.reshape(blocks, batch, GATE_COLS).astype(
            jnp.bfloat16
        )
        give(g, 0, 16, 0, to_core, 16)
        grad_rows = dot_nt(grad_pre, w_in_ref[...])
        part_grad[g] = grad_rows.reshape(blocks, batch, width).astype(jnp.bfloat16)
        give(g, 1, 16, 0, to_core, 16)

    def scatter_plane(g):
        for h in (0, 1):
            took(g, h, 0, 16)
            add(g, h, 12, 12)
            give(g, h, 12, 20, second[h])
        for h in (0, 1):
            add(g, h, second_slot[h], second_slot[h])
            give(g, h, second_slot[h], 16, second[h])
        for h in (0, 1):
            add(g, h, first_slot[h], first_slot[h])
            add(g, h, 0, 0)

    def scatter_near(g):
        for h in (0, 1):
            took(g, h, 20)
            add(g, h, first_slot[h], 20)
            give(g, h, first_slot[h], 24, first[h])

    def scatter_z(g):
        for h in (0, 1):
            took(g, h, 16)
            add(g, h, 0, 16)
        for h in (0, 1):
            took(g, h, 24)
            add(g, h, 0, 24)
            for dz in (2, 3, 1):
                give(g, h, dz, 28 + dz, to_z[dz], 1)

    totals = ([], [])

    def scatter_end(g):
        for h in (0, 1):
            total = partial[h][g, 0].astype(jnp.float32)
            for dz in (1, 3, 2):
                took(g, h, 28 + dz, 1)
                total = total + landing[h][g, 28 + dz].astype(jnp.float32)
            totals[h].append(total)

    for g in range(batches):
        gather_z(g)
    gather_plane(0)
    gather_plane(1)
    gather_far(0)
    gather_plane(2)
    gather_core(0)
    gather_far(1)
    gather_end(0)
    load_in.wait()
    load_out.wait()
    compute(0)
    gather_core(1)
    gather_far(2)
    scatter_plane(0)
    gather_end(1)
    compute(1)
    gather_core(2)
    scatter_near(0)
    scatter_plane(1)
    gather_end(2)
    compute(2)
    scatter_z(0)
    scatter_near(1)
    scatter_plane(2)
    grad_out_ref[...] = dot_tn(hidden_buf[...], cot_buf[...])
    save_out = pltpu.make_async_copy(grad_out_ref, grad_out_hbm, local_sem.at[1])
    save_out.start()
    scatter_z(1)
    scatter_near(2)
    tiles = half // 128
    grad_in = dot_tn(rows_buf[...], pre_buf[...])
    for tile in range(tiles):
        for side in range(2):
            left = side * half + tile * 128
            grad_in_ref[pl.ds(tile * 2 + side, width, stride=2 * tiles), :] = grad_in[
                :, left : left + 128
            ]
    save_in = pltpu.make_async_copy(grad_in_ref, grad_in_hbm, local_sem.at[0])
    save_in.start()
    scatter_z(2)
    for g in range(batches):
        scatter_end(g)
    total_mixed = jnp.concatenate(totals[0], axis=0)
    mixed_ref[...] = total_mixed[:, :width].astype(jnp.bfloat16)
    grad_tok_ref[...] = jnp.concatenate(totals[1], axis=0).astype(jnp.bfloat16)
    by_expert = total_mixed[:, width:]
    lines = []
    for k in range(per_token):
        chosen = jnp.logical_and(ids[k] == col_expert, col < 2 * groups)
        value = jnp.sum(jnp.where(chosen, by_expert, 0.0), axis=1, keepdims=True)
        lines.append(jnp.sum(jnp.where(diagonal, value, 0.0), axis=0, keepdims=True))
    grad_gates_ref[...] = jnp.concatenate(lines, axis=0)
    save_out.wait()
    save_in.wait()
    for copy in sent:
        copy.wait_send()


def dense_plan(tokens, grad_out, expert_ids, gates, w_in, w_out):
    count, width = tokens.shape
    groups = lax.axis_size("expert")
    half = w_out.shape[1]
    devices = 2 * groups
    batch = 8
    batches = count // batch
    vmem = pl.BlockSpec(memory_space=pltpu.VMEM)
    anywhere = pl.BlockSpec(memory_space=pl.ANY)
    total_rows = devices * count
    wide = width + GATE_COLS
    tiles = half // 128
    outs = pl.pallas_call(
        functools.partial(moe_kernel, groups),
        out_shape=(
            jax.ShapeDtypeStruct((count, width), jnp.bfloat16),
            jax.ShapeDtypeStruct((count, width), jnp.bfloat16),
            jax.ShapeDtypeStruct(gates.shape[::-1], jnp.float32),
            jax.ShapeDtypeStruct((width * 2 * tiles, 128), jnp.float32),
            jax.ShapeDtypeStruct((half, width), jnp.float32),
        ),
        in_specs=[vmem] * 4 + [anywhere] * 2,
        out_specs=[vmem] * 3 + [anywhere] * 2,
        scratch_shapes=[
            pltpu.VMEM((batches, devices, batch, wide), jnp.bfloat16),
            pltpu.VMEM((batches, devices, batch, width), jnp.bfloat16),
            pltpu.VMEM((batches, devices, batch, wide), jnp.bfloat16),
            pltpu.VMEM((batches, devices, batch, width), jnp.bfloat16),
            pltpu.VMEM((batches, devices, batch, wide), jnp.bfloat16),
            pltpu.VMEM((batches, devices, batch, width), jnp.bfloat16),
            pltpu.VMEM((total_rows, width), jnp.bfloat16),
            pltpu.VMEM((total_rows, width), jnp.bfloat16),
            pltpu.VMEM((total_rows, half), jnp.bfloat16),
            pltpu.VMEM((total_rows, 2 * half), jnp.bfloat16),
            pltpu.VMEM((width, 2 * half), jnp.bfloat16),
            pltpu.VMEM((half, width), jnp.bfloat16),
            pltpu.VMEM((width * 2 * tiles, 128), jnp.float32),
            pltpu.VMEM((half, width), jnp.float32),
            pltpu.SemaphoreType.DMA((batches, 2, devices)),
            pltpu.SemaphoreType.DMA((batches, 2, devices)),
            pltpu.SemaphoreType.DMA((batches, 2, devices)),
            pltpu.SemaphoreType.DMA((batches, 2, devices)),
            pltpu.SemaphoreType.DMA((2,)),
        ],
        compiler_params=pltpu.CompilerParams(
            collective_id=0, has_side_effects=True, vmem_limit_bytes=44 * 1024 * 1024
        ),
        cost_estimate=pl.CostEstimate(
            flops=18 * total_rows * width * half,
            bytes_accessed=12 * width * half + 6 * width * half,
            transcendentals=total_rows * half,
        ),
    )(tokens, grad_out, expert_ids.T, gates.T, w_in.reshape(width, 2 * half), w_out[0])
    mixed, grad_tokens, grad_gates, grad_in, grad_out_w = outs
    grad_in = grad_in.reshape(width, tiles, 2, 128).transpose(0, 2, 1, 3).reshape(w_in.shape)
    return (mixed, grad_tokens, grad_gates.T, grad_in, grad_out_w[None])


def per_device(tokens, grad_out, expert_ids, gates, w_in, w_out):
    if lax.axis_size("expert") == 16 and lax.axis_size("dp") == 2:
        return dense_plan(tokens, grad_out, expert_ids, gates, w_in, w_out)
    return routed_plan(tokens, grad_out, expert_ids, gates, w_in, w_out)


def solution(mesh):
    in_specs = (
        P(("dp", "expert"), None),
        P(("dp", "expert"), None),
        P(("dp", "expert"), None),
        P(("dp", "expert"), None),
        P("expert", None, None, "dp"),
        P("expert", "dp", None),
    )
    out_specs = (
        P(("dp", "expert"), None),
        P(("dp", "expert"), None),
        P(("dp", "expert"), None),
        P("expert", None, None, "dp"),
        P("expert", "dp", None),
    )
    return jax.shard_map(
        per_device, mesh=mesh, in_specs=in_specs, out_specs=out_specs, check_vma=False
    )
```

```python
import functools

import jax
import jax.numpy as jnp
from jax import lax
from jax.experimental import pallas as pl
from jax.experimental.pallas import tpu as pltpu
from jax.sharding import PartitionSpec as P


def forward_part(rows, weight_in, weight_out):
    model_width = rows.shape[1]
    hidden_width = weight_out.shape[0]
    flat_in = weight_in.reshape(model_width, 2 * hidden_width)
    preact = jnp.dot(rows, flat_in, preferred_element_type=jnp.float32)
    gate_part = preact[:, :hidden_width]
    up_part = preact[:, hidden_width:]
    activated = gate_part * jax.nn.sigmoid(gate_part)
    hidden = (activated * up_part).astype(jnp.bfloat16)
    result = jnp.dot(hidden, weight_out, preferred_element_type=jnp.float32).astype(jnp.bfloat16)
    return (preact, hidden, result)


def backward_part(rows, preact, hidden, grad_rows, weight_in, weight_out):
    model_width = rows.shape[1]
    hidden_width = weight_out.shape[0]
    flat_in = weight_in.reshape(model_width, 2 * hidden_width)
    gate_part = preact[:, :hidden_width]
    up_part = preact[:, hidden_width:]
    sigmoid_gate = jax.nn.sigmoid(gate_part)
    activated = gate_part * sigmoid_gate
    back_grad = jnp.einsum("sd,hd->sh", grad_rows, weight_out, preferred_element_type=jnp.float32)
    grad_gate = back_grad * up_part * (sigmoid_gate * (1.0 + gate_part * (1.0 - sigmoid_gate)))
    grad_up = back_grad * activated
    grad_pre = jnp.concatenate([grad_gate, grad_up], axis=1).astype(jnp.bfloat16)
    grad_rows_in = jnp.einsum(
        "sk,dk->sd", grad_pre, flat_in, preferred_element_type=jnp.float32
    ).astype(jnp.bfloat16)
    grad_weight_in = jnp.einsum("sd,sk->dk", rows, grad_pre, preferred_element_type=jnp.float32)
    grad_weight_out = jnp.einsum("sh,sd->hd", hidden, grad_rows, preferred_element_type=jnp.float32)
    return (grad_rows_in, grad_weight_in, grad_weight_out)


def routed_plan(tokens, grad_out, expert_ids, gates, w_in, w_out):
    count_tok, model_width = tokens.shape
    per_token = expert_ids.shape[1]
    groups = lax.axis_size("expert")
    capacity = min(count_tok, 3 * count_tok * per_token // (2 * groups))
    row_count = count_tok * per_token
    flat_ids = expert_ids.reshape(-1)
    onehot = (flat_ids[:, None] == jnp.arange(groups, dtype=jnp.int32)[None, :]).astype(jnp.int32)
    order_rank = jnp.sum((jnp.cumsum(onehot, axis=0) - onehot) * onehot, axis=1)
    slot_of_row = flat_ids * capacity + order_rank
    inverse = (
        jnp.full((groups * capacity,), row_count, jnp.int32)
        .at[slot_of_row]
        .set(jnp.arange(row_count, dtype=jnp.int32))
    )
    token_of_slot = jnp.where(inverse < row_count, inverse // per_token, count_tok)
    tokens_padded = jnp.concatenate([tokens, jnp.zeros((1, model_width), jnp.bfloat16)], axis=0)
    grad_padded = jnp.concatenate([grad_out, jnp.zeros((1, model_width), jnp.bfloat16)], axis=0)
    gates_padded = jnp.concatenate([gates.reshape(-1), jnp.zeros((1,), jnp.float32)], axis=0)
    send_rows = tokens_padded[token_of_slot].reshape(groups, capacity, model_width)
    slot_gate = gates_padded[inverse]
    send_grads = (slot_gate[:, None] * grad_padded[token_of_slot].astype(jnp.float32)).astype(
        jnp.bfloat16
    )
    send_grads = send_grads.reshape(groups, capacity, model_width)
    full_in, full_out = (
        lax.all_gather(w_in, "dp", axis=3, tiled=True),
        lax.all_gather(w_out, "dp", axis=1, tiled=True),
    )
    weight_in = full_in[0]
    weight_out = full_out[0]
    hidden_width = weight_out.shape[0]
    arrived_rows = lax.all_to_all(send_rows, "expert", split_axis=0, concat_axis=0, tiled=True)
    rows = arrived_rows.reshape(groups * capacity, model_width)
    preact, hidden, result = forward_part(rows, weight_in, weight_out)
    back_out = lax.all_to_all(
        result.reshape(groups, capacity, model_width),
        "expert",
        split_axis=0,
        concat_axis=0,
        tiled=True,
    )
    arrived_grads = lax.all_to_all(send_grads, "expert", split_axis=0, concat_axis=0, tiled=True)
    grad_rows = arrived_grads.reshape(groups * capacity, model_width)
    grad_rows_in, grad_weight_in, grad_weight_out = backward_part(
        rows, preact, hidden, grad_rows, weight_in, weight_out
    )
    back_grads = lax.all_to_all(
        grad_rows_in.reshape(groups, capacity, model_width),
        "expert",
        split_axis=0,
        concat_axis=0,
        tiled=True,
    )
    out_rows = back_out.reshape(groups * capacity, model_width)[slot_of_row].reshape(
        count_tok, per_token, model_width
    )
    mixed = jnp.sum(gates[:, :, None] * out_rows.astype(jnp.float32), axis=1).astype(jnp.bfloat16)
    grad_gates = jnp.einsum("td,tkd->tk", grad_out, out_rows, preferred_element_type=jnp.float32)
    route_dx = back_grads.reshape(groups * capacity, model_width)[slot_of_row].reshape(
        count_tok, per_token, model_width
    )
    grad_tokens = jnp.sum(route_dx.astype(jnp.float32), axis=1).astype(jnp.bfloat16)
    grad_in_shard, grad_out_shard = (
        lax.psum_scatter(
            grad_weight_in.reshape(1, model_width, 2, hidden_width).astype(jnp.bfloat16),
            "dp",
            scatter_dimension=3,
            tiled=True,
        ).astype(jnp.float32),
        lax.psum_scatter(
            grad_weight_out[None].astype(jnp.bfloat16), "dp", scatter_dimension=1, tiled=True
        ).astype(jnp.float32),
    )
    return (mixed, grad_tokens, grad_gates, grad_in_shard, grad_out_shard)


MESH = pl.DeviceIdType.MESH
GATE_COLS = 128


def dot_nt(a, b):
    return lax.dot_general(a, b, (((1,), (1,)), ((), ())), preferred_element_type=jnp.float32)


def dot_tn(a, b):
    return lax.dot_general(a, b, (((0,), (0,)), ((), ())), preferred_element_type=jnp.float32)


def moe_kernel(
    groups, tokens_ref, cot_ref, ids_ref, gates_ref, w_in_hbm, w_out_hbm,
    mixed_ref, grad_tok_ref, grad_gates_ref, grad_in_hbm, grad_out_hbm,
    tok_all, cot_all, part_mixed, part_grad, recv_mixed, recv_grad,
    rows_buf, cot_buf, hidden_buf, pre_buf, w_in_ref, w_out_ref, grad_in_ref, grad_out_ref,
    gather_send, gather_recv, scatter_send, scatter_recv, local_sem,
):
    count, width = tokens_ref.shape
    per_token = ids_ref.shape[0]
    half = w_out_ref.shape[0]
    batches, blocks, batch = tok_all.shape[:3]
    chunk = blocks * batch
    x = lax.axis_index("dp")
    e = lax.axis_index("expert")
    z, y, c = e // 4, (e // 2) % 2, e % 2

    def place(px, pz, py, pc):
        return (px, pz * 4 + py * 2 + pc)

    to_z = {
        1: place(x, z + 1 - 2 * (z % 2), y, c),
        2: place(x, (z + 2) % 4, y, c),
        3: place(x, 3 - z, y, c),
    }
    to_x = place(1 - x, z, y, c)
    to_y = place(x, z, 1 - y, c)
    to_core = place(x, z, y, 1 - c)

    partners = [to_z[1], to_z[2], to_z[3], to_x, to_y, to_core]
    barrier = pltpu.get_barrier_semaphore()
    for partner in partners:
        pl.semaphore_signal(barrier, inc=1, device_id=partner, device_id_type=MESH)
    load_in = pltpu.make_async_copy(w_in_hbm, w_in_ref, local_sem.at[0])
    load_out = pltpu.make_async_copy(w_out_hbm, w_out_ref, local_sem.at[1])
    load_in.start()
    load_out.start()

    col = lax.broadcasted_iota(jnp.int32, (count, GATE_COLS), 1)
    col_expert = (col % groups).astype(jnp.float32)
    diagonal = lax.broadcasted_iota(jnp.int32, (count, count), 0) == lax.broadcasted_iota(
        jnp.int32, (count, count), 1
    )
    ids_t = ids_ref[...].astype(jnp.float32)
    gates_t = gates_ref[...]

    def column(table, k):
        return jnp.sum(jnp.where(diagonal, table[k : k + 1, :], 0.0), axis=1, keepdims=True)

    ids = [column(ids_t, k) for k in range(per_token)]
    dense = jnp.zeros((count, GATE_COLS), jnp.float32)
    for k in range(per_token):
        dense = dense + jnp.where(ids[k] == col_expert, column(gates_t, k), 0.0)
    high = dense.astype(jnp.bfloat16).astype(jnp.float32)
    middle = (dense - high).astype(jnp.bfloat16).astype(jnp.float32)
    low = dense - high - middle
    pieces = jnp.where(
        col < groups,
        high,
        jnp.where(col < 2 * groups, middle, jnp.where(col < 3 * groups, low, 0.0)),
    )
    own_tokens = tokens_ref[...].astype(jnp.float32)
    own_cot = cot_ref[...].astype(jnp.float32)
    for g in range(batches):
        part = slice(g * batch, (g + 1) * batch)
        tok_all[g, 0, :, :width] = own_tokens[part].astype(jnp.bfloat16)
        tok_all[g, 0, :, width:] = pieces[part].astype(jnp.bfloat16)
        cot_all[g, 0] = own_cot[part].astype(jnp.bfloat16)
    pl.semaphore_wait(barrier, len(partners))

    gathered = (tok_all, cot_all)
    partial = (part_mixed, part_grad)
    landing = (recv_mixed, recv_grad)
    sent = []

    def copy_of(source, target, sems, g, h, src, dst, device, number):
        return pltpu.make_async_remote_copy(
            src_ref=source[h].at[g, pl.ds(src, number)],
            dst_ref=target[h].at[g, pl.ds(dst, number)],
            send_sem=sems[0].at[g, h, dst],
            recv_sem=sems[1].at[g, h, dst],
            device_id=device,
            device_id_type=MESH,
        )

    gather_sems = (gather_send, gather_recv)
    scatter_sems = (scatter_send, scatter_recv)

    def push(g, h, src, dst, device, number=4):
        copy = copy_of(gathered, gathered, gather_sems, g, h, src, dst, device, number)
        copy.start()
        sent.append(copy)

    def arrived(g, h, slot, number=4):
        copy_of(gathered, gathered, gather_sems, g, h, slot, slot, to_core, number).wait_recv()

    def give(g, h, src, dst, device, number=4):
        copy = copy_of(partial, landing, scatter_sems, g, h, src, dst, device, number)
        copy.start()
        sent.append(copy)

    def took(g, h, dst, number=4):
        copy_of(partial, landing, scatter_sems, g, h, 0, dst, to_core, number).wait_recv()

    def add(g, h, slot, dst, number=4):
        here = pl.ds(slot, number)
        partial[h][g, here] = (
            partial[h][g, here].astype(jnp.float32)
            + landing[h][g, pl.ds(dst, number)].astype(jnp.float32)
        ).astype(jnp.bfloat16)

    first = (to_x, to_y)
    second = (to_y, to_x)
    first_slot = (8, 4)
    second_slot = (4, 8)

    plane_first = [g == 1 for g in range(batches)]

    def gather_z(g):
        for dz in (1, 3, 2):
            for h in (0, 1):
                push(g, h, 0, dz, to_z[dz], 1)

    def gather_own(g):
        for h in (0, 1):
            push(g, h, 0, first_slot[h], first[h], 1)
        if not plane_first[g]:
            for h in (0, 1):
                push(g, h, 0, second_slot[h], second[h], 1)

    def gather_plane(g):
        if plane_first[g]:
            for h in (0, 1):
                slot = first_slot[h]
                arrived(g, h, slot, 1)
                for dz in (1, 3, 2):
                    push(g, h, slot, slot + dz, to_z[dz], 1)
        for h in (0, 1):
            for dz in (1, 3, 2):
                arrived(g, h, dz, 1)
            if plane_first[g]:
                push(g, h, 0, second_slot[h], second[h])
            else:
                push(g, h, 1, first_slot[h] + 1, first[h], 3)
                push(g, h, 1, second_slot[h] + 1, second[h], 3)
            push(g, h, 0, 16, to_core)

    def gather_far(g):
        for h in (0, 1):
            slot = first_slot[h]
            if plane_first[g]:
                for dz in (1, 3, 2):
                    arrived(g, h, slot + dz, 1)
            else:
                arrived(g, h, slot, 1)
                arrived(g, h, slot + 1, 3)
            push(g, h, slot, 12, second[h])
            push(g, h, slot, 16 + slot, to_core)

    def gather_core(g):
        for h in (0, 1):
            slot = second_slot[h]
            if plane_first[g]:
                arrived(g, h, slot)
            else:
                arrived(g, h, slot, 1)
                arrived(g, h, slot + 1, 3)
            push(g, h, slot, 16 + slot, to_core)
        for h in (0, 1):
            arrived(g, h, 12)
            push(g, h, 12, 28, to_core)

    def gather_end(g):
        for slot in (16, 20, 24, 28):
            for h in (0, 1):
                arrived(g, h, slot)

    wide_col = lax.broadcasted_iota(jnp.int32, (chunk, GATE_COLS), 1)

    def compute(g):
        here = pl.ds(chunk * g, chunk)
        packed = tok_all[g].astype(jnp.float32).reshape(chunk, width + GATE_COLS)
        rows = packed[:, :width].astype(jnp.bfloat16)
        cot = cot_all[g].astype(jnp.float32).reshape(chunk, width).astype(jnp.bfloat16)
        own = jnp.logical_and(wide_col % groups == e, wide_col < 3 * groups)
        gate = jnp.sum(jnp.where(own, packed[:, width:], 0.0), axis=1, keepdims=True)
        rows_buf[here, :] = rows
        cot_buf[here, :] = cot
        preact = jnp.dot(rows, w_in_ref[...], preferred_element_type=jnp.float32)
        gate_part = preact[:, :half]
        up_part = preact[:, half:]
        sig = jax.nn.sigmoid(gate_part)
        activated = gate_part * sig
        hidden = activated * up_part
        back = dot_nt(cot, w_out_ref[...])
        gate_grad = jnp.sum(hidden * back, axis=1, keepdims=True)
        gated_hidden = (gate * hidden).astype(jnp.bfloat16)
        gated_back = gate * back
        grad_gate = gated_back * up_part * (sig * (1.0 + gate_part * (1.0 - sig)))
        grad_up = gated_back * activated
        grad_pre = jnp.concatenate([grad_gate, grad_up], axis=1).astype(jnp.bfloat16)
        hidden_buf[here, :] = gated_hidden
        pre_buf[here, :] = grad_pre
        mixed = jnp.dot(gated_hidden, w_out_ref[...], preferred_element_type=jnp.float32)
        part_mixed[g, :, :, :width] = mixed.reshape(blocks, batch, width).astype(jnp.bfloat16)
        high = gate_grad.astype(jnp.bfloat16).astype(jnp.float32)
        spread = jnp.where(
            wide_col == e, high, jnp.where(wide_col == groups + e, gate_grad - high, 0.0)
        )
        part_mixed[g, :, :, width:] = spread.reshape(blocks, batch, GATE_COLS).astype(
            jnp.bfloat16
        )
        give(g, 0, 16, 0, to_core, 16)
        grad_rows = dot_nt(grad_pre, w_in_ref[...])
        part_grad[g] = grad_rows.reshape(blocks, batch, width).astype(jnp.bfloat16)
        give(g, 1, 16, 0, to_core, 16)

    def scatter_plane(g):
        for h in (0, 1):
            took(g, h, 0, 16)
            add(g, h, 12, 12)
            give(g, h, 12, 20, second[h])
        for h in (0, 1):
            add(g, h, second_slot[h], second_slot[h])
            give(g, h, second_slot[h], 16, second[h])
        for h in (0, 1):
            add(g, h, first_slot[h], first_slot[h])
            add(g, h, 0, 0)

    def scatter_near(g):
        for h in (0, 1):
            slot = first_slot[h]
            took(g, h, 20)
            add(g, h, slot, 20)
            if plane_first[g]:
                for dz in (2, 3, 1):
                    give(g, h, slot + dz, 24 + dz, to_z[dz], 1)
            else:
                give(g, h, slot, 24, first[h])

    def scatter_z(g):
        for h in (0, 1):
            took(g, h, 16)
            add(g, h, 0, 16)
            if plane_first[g]:
                for dz in (2, 3, 1):
                    give(g, h, dz, 28 + dz, to_z[dz], 1)
        for h in (0, 1):
            if plane_first[g]:
                slot = first_slot[h]
                for dz in (1, 3, 2):
                    took(g, h, 24 + dz, 1)
                total = partial[h][g, slot].astype(jnp.float32)
                for dz in (1, 3, 2):
                    total = total + landing[h][g, 24 + dz].astype(jnp.float32)
                partial[h][g, slot] = total.astype(jnp.bfloat16)
                give(g, h, slot, 24, first[h], 1)
            else:
                took(g, h, 24)
                add(g, h, 0, 24)
                for dz in (2, 3, 1):
                    give(g, h, dz, 28 + dz, to_z[dz], 1)

    totals = ([], [])

    def scatter_end(g):
        for h in (0, 1):
            total = partial[h][g, 0].astype(jnp.float32)
            for dz in (1, 3, 2):
                took(g, h, 28 + dz, 1)
                total = total + landing[h][g, 28 + dz].astype(jnp.float32)
            if plane_first[g]:
                took(g, h, 24, 1)
                total = total + landing[h][g, 24].astype(jnp.float32)
            totals[h].append(total)

    tiles = half // 128

    def weight_out(lower, upper, more):
        part = pl.ds(lower * chunk, (upper - lower) * chunk)
        value = dot_tn(hidden_buf[part, :], cot_buf[part, :])
        grad_out_ref[...] = grad_out_ref[...] + value if more else value

    def weight_in(lower, upper, more):
        part = pl.ds(lower * chunk, (upper - lower) * chunk)
        value = dot_tn(rows_buf[part, :], pre_buf[part, :])
        for tile in range(tiles):
            for side in range(2):
                left = side * half + tile * 128
                where = pl.ds(tile * 2 + side, width, stride=2 * tiles)
                piece = value[:, left : left + 128]
                grad_in_ref[where, :] = grad_in_ref[where, :] + piece if more else piece

    gather_z(0)
    gather_own(1)
    gather_own(0)
    gather_z(1)
    gather_own(2)
    gather_z(2)
    gather_plane(0)
    gather_plane(1)
    gather_far(0)
    gather_plane(2)
    gather_core(0)
    gather_far(1)
    gather_end(0)
    load_in.wait()
    load_out.wait()
    compute(0)
    gather_core(1)
    gather_far(2)
    scatter_plane(0)
    gather_end(1)
    compute(1)
    gather_core(2)
    scatter_near(0)
    scatter_plane(1)
    weight_out(0, 2, False)
    weight_in(0, 2, False)
    gather_end(2)
    compute(2)
    scatter_z(0)
    scatter_near(1)
    scatter_plane(2)
    weight_out(2, 3, True)
    save_out = pltpu.make_async_copy(grad_out_ref, grad_out_hbm, local_sem.at[1])
    save_out.start()
    scatter_near(2)
    scatter_z(1)
    weight_in(2, 3, True)
    save_in = pltpu.make_async_copy(grad_in_ref, grad_in_hbm, local_sem.at[0])
    save_in.start()
    scatter_z(2)
    for g in range(batches):
        scatter_end(g)
    total_mixed = jnp.concatenate(totals[0], axis=0)
    mixed_ref[...] = total_mixed[:, :width].astype(jnp.bfloat16)
    grad_tok_ref[...] = jnp.concatenate(totals[1], axis=0).astype(jnp.bfloat16)
    by_expert = total_mixed[:, width:]
    lines = []
    for k in range(per_token):
        chosen = jnp.logical_and(ids[k] == col_expert, col < 2 * groups)
        value = jnp.sum(jnp.where(chosen, by_expert, 0.0), axis=1, keepdims=True)
        lines.append(jnp.sum(jnp.where(diagonal, value, 0.0), axis=0, keepdims=True))
    grad_gates_ref[...] = jnp.concatenate(lines, axis=0)
    save_out.wait()
    save_in.wait()
    for copy in sent:
        copy.wait_send()


def dense_plan(tokens, grad_out, expert_ids, gates, w_in, w_out):
    count, width = tokens.shape
    groups = lax.axis_size("expert")
    half = w_out.shape[1]
    devices = 2 * groups
    batch = 8
    batches = count // batch
    vmem = pl.BlockSpec(memory_space=pltpu.VMEM)
    anywhere = pl.BlockSpec(memory_space=pl.ANY)
    total_rows = devices * count
    wide = width + GATE_COLS
    tiles = half // 128
    outs = pl.pallas_call(
        functools.partial(moe_kernel, groups),
        out_shape=(
            jax.ShapeDtypeStruct((count, width), jnp.bfloat16),
            jax.ShapeDtypeStruct((count, width), jnp.bfloat16),
            jax.ShapeDtypeStruct(gates.shape[::-1], jnp.float32),
            jax.ShapeDtypeStruct((width * 2 * tiles, 128), jnp.float32),
            jax.ShapeDtypeStruct((half, width), jnp.float32),
        ),
        in_specs=[vmem] * 4 + [anywhere] * 2,
        out_specs=[vmem] * 3 + [anywhere] * 2,
        scratch_shapes=[
            pltpu.VMEM((batches, devices, batch, wide), jnp.bfloat16),
            pltpu.VMEM((batches, devices, batch, width), jnp.bfloat16),
            pltpu.VMEM((batches, devices, batch, wide), jnp.bfloat16),
            pltpu.VMEM((batches, devices, batch, width), jnp.bfloat16),
            pltpu.VMEM((batches, devices, batch, wide), jnp.bfloat16),
            pltpu.VMEM((batches, devices, batch, width), jnp.bfloat16),
            pltpu.VMEM((total_rows, width), jnp.bfloat16),
            pltpu.VMEM((total_rows, width), jnp.bfloat16),
            pltpu.VMEM((total_rows, half), jnp.bfloat16),
            pltpu.VMEM((total_rows, 2 * half), jnp.bfloat16),
            pltpu.VMEM((width, 2 * half), jnp.bfloat16),
            pltpu.VMEM((half, width), jnp.bfloat16),
            pltpu.VMEM((width * 2 * tiles, 128), jnp.float32),
            pltpu.VMEM((half, width), jnp.float32),
            pltpu.SemaphoreType.DMA((batches, 2, devices)),
            pltpu.SemaphoreType.DMA((batches, 2, devices)),
            pltpu.SemaphoreType.DMA((batches, 2, devices)),
            pltpu.SemaphoreType.DMA((batches, 2, devices)),
            pltpu.SemaphoreType.DMA((2,)),
        ],
        compiler_params=pltpu.CompilerParams(
            collective_id=0, has_side_effects=True, vmem_limit_bytes=44 * 1024 * 1024
        ),
        cost_estimate=pl.CostEstimate(
            flops=18 * total_rows * width * half,
            bytes_accessed=12 * width * half + 6 * width * half,
            transcendentals=total_rows * half,
        ),
    )(tokens, grad_out, expert_ids.T, gates.T, w_in.reshape(width, 2 * half), w_out[0])
    mixed, grad_tokens, grad_gates, grad_in, grad_out_w = outs
    grad_in = grad_in.reshape(width, tiles, 2, 128).transpose(0, 2, 1, 3).reshape(w_in.shape)
    return (mixed, grad_tokens, grad_gates.T, grad_in, grad_out_w[None])


def per_device(tokens, grad_out, expert_ids, gates, w_in, w_out):
    if lax.axis_size("expert") == 16 and lax.axis_size("dp") == 2:
        return dense_plan(tokens, grad_out, expert_ids, gates, w_in, w_out)
    return routed_plan(tokens, grad_out, expert_ids, gates, w_in, w_out)


def solution(mesh):
    in_specs = (
        P(("dp", "expert"), None),
        P(("dp", "expert"), None),
        P(("dp", "expert"), None),
        P(("dp", "expert"), None),
        P("expert", None, None, "dp"),
        P("expert", "dp", None),
    )
    out_specs = (
        P(("dp", "expert"), None),
        P(("dp", "expert"), None),
        P(("dp", "expert"), None),
        P("expert", None, None, "dp"),
        P("expert", "dp", None),
    )
    return jax.shard_map(
        per_device, mesh=mesh, in_specs=in_specs, out_specs=out_specs, check_vma=False
    )
```

```python
import functools

import jax
import jax.numpy as jnp
from jax import lax
from jax.experimental import pallas as pl
from jax.experimental.pallas import tpu as pltpu
from jax.sharding import PartitionSpec as P


def forward_part(rows, weight_in, weight_out):
    model_width = rows.shape[1]
    hidden_width = weight_out.shape[0]
    flat_in = weight_in.reshape(model_width, 2 * hidden_width)
    preact = jnp.dot(rows, flat_in, preferred_element_type=jnp.float32)
    gate_part = preact[:, :hidden_width]
    up_part = preact[:, hidden_width:]
    activated = gate_part * jax.nn.sigmoid(gate_part)
    hidden = (activated * up_part).astype(jnp.bfloat16)
    result = jnp.dot(hidden, weight_out, preferred_element_type=jnp.float32).astype(jnp.bfloat16)
    return (preact, hidden, result)


def backward_part(rows, preact, hidden, grad_rows, weight_in, weight_out):
    model_width = rows.shape[1]
    hidden_width = weight_out.shape[0]
    flat_in = weight_in.reshape(model_width, 2 * hidden_width)
    gate_part = preact[:, :hidden_width]
    up_part = preact[:, hidden_width:]
    sigmoid_gate = jax.nn.sigmoid(gate_part)
    activated = gate_part * sigmoid_gate
    back_grad = jnp.einsum("sd,hd->sh", grad_rows, weight_out, preferred_element_type=jnp.float32)
    grad_gate = back_grad * up_part * (sigmoid_gate * (1.0 + gate_part * (1.0 - sigmoid_gate)))
    grad_up = back_grad * activated
    grad_pre = jnp.concatenate([grad_gate, grad_up], axis=1).astype(jnp.bfloat16)
    grad_rows_in = jnp.einsum(
        "sk,dk->sd", grad_pre, flat_in, preferred_element_type=jnp.float32
    ).astype(jnp.bfloat16)
    grad_weight_in = jnp.einsum("sd,sk->dk", rows, grad_pre, preferred_element_type=jnp.float32)
    grad_weight_out = jnp.einsum("sh,sd->hd", hidden, grad_rows, preferred_element_type=jnp.float32)
    return (grad_rows_in, grad_weight_in, grad_weight_out)


def routed_plan(tokens, grad_out, expert_ids, gates, w_in, w_out):
    count_tok, model_width = tokens.shape
    per_token = expert_ids.shape[1]
    groups = lax.axis_size("expert")
    capacity = min(count_tok, 3 * count_tok * per_token // (2 * groups))
    row_count = count_tok * per_token
    flat_ids = expert_ids.reshape(-1)
    onehot = (flat_ids[:, None] == jnp.arange(groups, dtype=jnp.int32)[None, :]).astype(jnp.int32)
    order_rank = jnp.sum((jnp.cumsum(onehot, axis=0) - onehot) * onehot, axis=1)
    slot_of_row = flat_ids * capacity + order_rank
    inverse = (
        jnp.full((groups * capacity,), row_count, jnp.int32)
        .at[slot_of_row]
        .set(jnp.arange(row_count, dtype=jnp.int32))
    )
    token_of_slot = jnp.where(inverse < row_count, inverse // per_token, count_tok)
    tokens_padded = jnp.concatenate([tokens, jnp.zeros((1, model_width), jnp.bfloat16)], axis=0)
    grad_padded = jnp.concatenate([grad_out, jnp.zeros((1, model_width), jnp.bfloat16)], axis=0)
    gates_padded = jnp.concatenate([gates.reshape(-1), jnp.zeros((1,), jnp.float32)], axis=0)
    send_rows = tokens_padded[token_of_slot].reshape(groups, capacity, model_width)
    slot_gate = gates_padded[inverse]
    send_grads = (slot_gate[:, None] * grad_padded[token_of_slot].astype(jnp.float32)).astype(
        jnp.bfloat16
    )
    send_grads = send_grads.reshape(groups, capacity, model_width)
    full_in, full_out = (
        lax.all_gather(w_in, "dp", axis=3, tiled=True),
        lax.all_gather(w_out, "dp", axis=1, tiled=True),
    )
    weight_in = full_in[0]
    weight_out = full_out[0]
    hidden_width = weight_out.shape[0]
    arrived_rows = lax.all_to_all(send_rows, "expert", split_axis=0, concat_axis=0, tiled=True)
    rows = arrived_rows.reshape(groups * capacity, model_width)
    preact, hidden, result = forward_part(rows, weight_in, weight_out)
    back_out = lax.all_to_all(
        result.reshape(groups, capacity, model_width),
        "expert",
        split_axis=0,
        concat_axis=0,
        tiled=True,
    )
    arrived_grads = lax.all_to_all(send_grads, "expert", split_axis=0, concat_axis=0, tiled=True)
    grad_rows = arrived_grads.reshape(groups * capacity, model_width)
    grad_rows_in, grad_weight_in, grad_weight_out = backward_part(
        rows, preact, hidden, grad_rows, weight_in, weight_out
    )
    back_grads = lax.all_to_all(
        grad_rows_in.reshape(groups, capacity, model_width),
        "expert",
        split_axis=0,
        concat_axis=0,
        tiled=True,
    )
    out_rows = back_out.reshape(groups * capacity, model_width)[slot_of_row].reshape(
        count_tok, per_token, model_width
    )
    mixed = jnp.sum(gates[:, :, None] * out_rows.astype(jnp.float32), axis=1).astype(jnp.bfloat16)
    grad_gates = jnp.einsum("td,tkd->tk", grad_out, out_rows, preferred_element_type=jnp.float32)
    route_dx = back_grads.reshape(groups * capacity, model_width)[slot_of_row].reshape(
        count_tok, per_token, model_width
    )
    grad_tokens = jnp.sum(route_dx.astype(jnp.float32), axis=1).astype(jnp.bfloat16)
    grad_in_shard, grad_out_shard = (
        lax.psum_scatter(
            grad_weight_in.reshape(1, model_width, 2, hidden_width).astype(jnp.bfloat16),
            "dp",
            scatter_dimension=3,
            tiled=True,
        ).astype(jnp.float32),
        lax.psum_scatter(
            grad_weight_out[None].astype(jnp.bfloat16), "dp", scatter_dimension=1, tiled=True
        ).astype(jnp.float32),
    )
    return (mixed, grad_tokens, grad_gates, grad_in_shard, grad_out_shard)


MESH = pl.DeviceIdType.MESH
GATE_COLS = 128


def dot_tn(a, b):
    return lax.dot_general(a, b, (((0,), (0,)), ((), ())), preferred_element_type=jnp.float32)


def moe_kernel(
    groups, tokens_ref, cot_ref, ids_ref, gates_ref, w_in_hbm, w_out_hbm,
    mixed_ref, grad_tok_ref, grad_gates_ref, grad_in_hbm, grad_out_hbm,
    tok_all, cot_all, part_mixed, part_grad, recv_mixed, recv_grad,
    rows_buf, cot_buf, hidden_buf, pre_buf, w_in_ref, w_out_ref, w_in_t, w_out_t,
    grad_in_ref, grad_out_ref,
    gather_send, gather_recv, scatter_send, scatter_recv, local_sem,
):
    count, width = tokens_ref.shape
    per_token = ids_ref.shape[0]
    half = w_out_ref.shape[0]
    batches, blocks, batch = tok_all.shape[:3]
    chunk = blocks * batch
    x = lax.axis_index("dp")
    e = lax.axis_index("expert")
    z, y, c = e // 4, (e // 2) % 2, e % 2

    def place(px, pz, py, pc):
        return (px, pz * 4 + py * 2 + pc)

    to_z = {
        1: place(x, z + 1 - 2 * (z % 2), y, c),
        2: place(x, (z + 2) % 4, y, c),
        3: place(x, 3 - z, y, c),
    }
    to_x = place(1 - x, z, y, c)
    to_y = place(x, z, 1 - y, c)
    to_core = place(x, z, y, 1 - c)

    partners = [to_z[1], to_z[2], to_z[3], to_x, to_y, to_core]
    barrier = pltpu.get_barrier_semaphore()
    for partner in partners:
        pl.semaphore_signal(barrier, inc=1, device_id=partner, device_id_type=MESH)
    load_in = pltpu.make_async_copy(w_in_hbm, w_in_ref, local_sem.at[0])
    load_out = pltpu.make_async_copy(w_out_hbm, w_out_ref, local_sem.at[1])
    load_in.start()
    load_out.start()

    col = lax.broadcasted_iota(jnp.int32, (count, GATE_COLS), 1)
    col_expert = (col % groups).astype(jnp.float32)
    diagonal = lax.broadcasted_iota(jnp.int32, (count, count), 0) == lax.broadcasted_iota(
        jnp.int32, (count, count), 1
    )
    ids_t = ids_ref[...].astype(jnp.float32)
    gates_t = gates_ref[...]

    def column(table, k):
        return jnp.sum(jnp.where(diagonal, table[k : k + 1, :], 0.0), axis=1, keepdims=True)

    ids = [column(ids_t, k) for k in range(per_token)]
    dense = jnp.zeros((count, GATE_COLS), jnp.float32)
    for k in range(per_token):
        dense = dense + jnp.where(ids[k] == col_expert, column(gates_t, k), 0.0)
    high = dense.astype(jnp.bfloat16).astype(jnp.float32)
    middle = (dense - high).astype(jnp.bfloat16).astype(jnp.float32)
    low = dense - high - middle
    pieces = jnp.where(
        col < groups,
        high,
        jnp.where(col < 2 * groups, middle, jnp.where(col < 3 * groups, low, 0.0)),
    )
    own_tokens = tokens_ref[...].astype(jnp.float32)
    own_cot = cot_ref[...].astype(jnp.float32)
    for g in range(batches):
        part = slice(g * batch, (g + 1) * batch)
        tok_all[g, 0, :, :width] = own_tokens[part].astype(jnp.bfloat16)
        tok_all[g, 0, :, width:] = pieces[part].astype(jnp.bfloat16)
        cot_all[g, 0] = own_cot[part].astype(jnp.bfloat16)
    pl.semaphore_wait(barrier, len(partners))

    gathered = (tok_all, cot_all)
    partial = (part_mixed, part_grad)
    landing = (recv_mixed, recv_grad)
    sent = []

    def copy_of(source, target, sems, g, h, src, dst, device, number):
        return pltpu.make_async_remote_copy(
            src_ref=source[h].at[g, pl.ds(src, number)],
            dst_ref=target[h].at[g, pl.ds(dst, number)],
            send_sem=sems[0].at[g, h, dst],
            recv_sem=sems[1].at[g, h, dst],
            device_id=device,
            device_id_type=MESH,
        )

    gather_sems = (gather_send, gather_recv)
    scatter_sems = (scatter_send, scatter_recv)

    def push(g, h, src, dst, device, number=4):
        copy = copy_of(gathered, gathered, gather_sems, g, h, src, dst, device, number)
        copy.start()
        sent.append(copy)

    def arrived(g, h, slot, number=4):
        copy_of(gathered, gathered, gather_sems, g, h, slot, slot, to_core, number).wait_recv()

    def give(g, h, src, dst, device, number=4):
        copy = copy_of(partial, landing, scatter_sems, g, h, src, dst, device, number)
        copy.start()
        sent.append(copy)

    def took(g, h, dst, number=4):
        copy_of(partial, landing, scatter_sems, g, h, 0, dst, to_core, number).wait_recv()

    def add(g, h, slot, dst, number=4):
        here = pl.ds(slot, number)
        partial[h][g, here] = (
            partial[h][g, here].astype(jnp.float32)
            + landing[h][g, pl.ds(dst, number)].astype(jnp.float32)
        ).astype(jnp.bfloat16)

    first = (to_x, to_y)
    second = (to_y, to_x)
    first_slot = (8, 4)
    second_slot = (4, 8)

    plane_first = [g == 1 for g in range(batches)]

    def gather_z(g):
        for dz in (1, 3, 2):
            for h in (0, 1):
                push(g, h, 0, dz, to_z[dz], 1)

    def gather_own(g):
        for h in (0, 1):
            push(g, h, 0, first_slot[h], first[h], 1)
        if not plane_first[g]:
            for h in (0, 1):
                push(g, h, 0, second_slot[h], second[h], 1)

    def gather_plane(g):
        if plane_first[g]:
            for h in (0, 1):
                slot = first_slot[h]
                arrived(g, h, slot, 1)
                for dz in (1, 3, 2):
                    push(g, h, slot, slot + dz, to_z[dz], 1)
        for h in (0, 1):
            for dz in (1, 3, 2):
                arrived(g, h, dz, 1)
            if plane_first[g]:
                push(g, h, 0, second_slot[h], second[h])
            else:
                push(g, h, 1, first_slot[h] + 1, first[h], 3)
                push(g, h, 1, second_slot[h] + 1, second[h], 3)
            push(g, h, 0, 16, to_core)

    def gather_far(g):
        for h in (0, 1):
            slot = first_slot[h]
            if plane_first[g]:
                for dz in (1, 3, 2):
                    arrived(g, h, slot + dz, 1)
            else:
                arrived(g, h, slot, 1)
                arrived(g, h, slot + 1, 3)
            push(g, h, slot, 12, second[h])
            push(g, h, slot, 16 + slot, to_core)

    def gather_core(g):
        for h in (0, 1):
            slot = second_slot[h]
            if plane_first[g]:
                arrived(g, h, slot)
            else:
                arrived(g, h, slot, 1)
                arrived(g, h, slot + 1, 3)
            push(g, h, slot, 16 + slot, to_core)
        for h in (0, 1):
            arrived(g, h, 12)
            push(g, h, 12, 28, to_core)

    def gather_end(g):
        for slot in (16, 20, 24, 28):
            for h in (0, 1):
                arrived(g, h, slot)

    wide_col = lax.broadcasted_iota(jnp.int32, (chunk, GATE_COLS), 1)

    def compute(g):
        here = pl.ds(chunk * g, chunk)
        packed = tok_all[g].astype(jnp.float32).reshape(chunk, width + GATE_COLS)
        rows = packed[:, :width].astype(jnp.bfloat16)
        cot = cot_all[g].astype(jnp.float32).reshape(chunk, width).astype(jnp.bfloat16)
        own = jnp.logical_and(wide_col % groups == e, wide_col < 3 * groups)
        gate = jnp.sum(jnp.where(own, packed[:, width:], 0.0), axis=1, keepdims=True)
        rows_buf[here, :] = rows
        cot_buf[here, :] = cot
        preact = jnp.dot(rows, w_in_ref[...], preferred_element_type=jnp.float32)
        gate_part = preact[:, :half]
        up_part = preact[:, half:]
        sig = jax.nn.sigmoid(gate_part)
        activated = gate_part * sig
        hidden = activated * up_part
        back = jnp.dot(cot, w_out_t[...], preferred_element_type=jnp.float32)
        gate_grad = jnp.sum(hidden * back, axis=1, keepdims=True)
        gated_hidden = (gate * hidden).astype(jnp.bfloat16)
        gated_back = gate * back
        grad_gate = gated_back * up_part * (sig * (1.0 + gate_part * (1.0 - sig)))
        grad_up = gated_back * activated
        grad_pre = jnp.concatenate([grad_gate, grad_up], axis=1).astype(jnp.bfloat16)
        hidden_buf[here, :] = gated_hidden
        pre_buf[here, :] = grad_pre
        mixed = jnp.dot(gated_hidden, w_out_ref[...], preferred_element_type=jnp.float32)
        part_mixed[g, :, :, :width] = mixed.reshape(blocks, batch, width).astype(jnp.bfloat16)
        high = gate_grad.astype(jnp.bfloat16).astype(jnp.float32)
        spread = jnp.where(
            wide_col == e, high, jnp.where(wide_col == groups + e, gate_grad - high, 0.0)
        )
        part_mixed[g, :, :, width:] = spread.reshape(blocks, batch, GATE_COLS).astype(
            jnp.bfloat16
        )
        give(g, 0, 16, 0, to_core, 16)
        grad_rows = jnp.dot(grad_pre, w_in_t[...], preferred_element_type=jnp.float32)
        part_grad[g] = grad_rows.reshape(blocks, batch, width).astype(jnp.bfloat16)
        give(g, 1, 16, 0, to_core, 16)

    def scatter_plane(g):
        for h in (0, 1):
            took(g, h, 0, 16)
            add(g, h, 12, 12)
            give(g, h, 12, 20, second[h])
        for h in (0, 1):
            add(g, h, second_slot[h], second_slot[h])
            give(g, h, second_slot[h], 16, second[h])
        for h in (0, 1):
            add(g, h, first_slot[h], first_slot[h])
            add(g, h, 0, 0)

    def scatter_near(g):
        for h in (0, 1):
            slot = first_slot[h]
            took(g, h, 20)
            add(g, h, slot, 20)
            if plane_first[g]:
                for dz in (2, 3, 1):
                    give(g, h, slot + dz, 24 + dz, to_z[dz], 1)
            else:
                give(g, h, slot, 24, first[h])

    def scatter_z(g):
        for h in (0, 1):
            took(g, h, 16)
            add(g, h, 0, 16)
            if plane_first[g]:
                for dz in (2, 3, 1):
                    give(g, h, dz, 28 + dz, to_z[dz], 1)
        for h in (0, 1):
            if plane_first[g]:
                slot = first_slot[h]
                for dz in (1, 3, 2):
                    took(g, h, 24 + dz, 1)
                total = partial[h][g, slot].astype(jnp.float32)
                for dz in (1, 3, 2):
                    total = total + landing[h][g, 24 + dz].astype(jnp.float32)
                partial[h][g, slot] = total.astype(jnp.bfloat16)
                give(g, h, slot, 24, first[h], 1)
            else:
                took(g, h, 24)
                add(g, h, 0, 24)
                for dz in (2, 3, 1):
                    give(g, h, dz, 28 + dz, to_z[dz], 1)

    totals = ([], [])

    def scatter_end(g):
        for h in (0, 1):
            total = partial[h][g, 0].astype(jnp.float32)
            for dz in (1, 3, 2):
                took(g, h, 28 + dz, 1)
                total = total + landing[h][g, 28 + dz].astype(jnp.float32)
            if plane_first[g]:
                took(g, h, 24, 1)
                total = total + landing[h][g, 24].astype(jnp.float32)
            totals[h].append(total)

    tiles = half // 128

    def weight_out(lower, upper, more):
        part = pl.ds(lower * chunk, (upper - lower) * chunk)
        value = dot_tn(hidden_buf[part, :], cot_buf[part, :])
        grad_out_ref[...] = grad_out_ref[...] + value if more else value

    def weight_in(lower, upper, more):
        part = pl.ds(lower * chunk, (upper - lower) * chunk)
        value = dot_tn(rows_buf[part, :], pre_buf[part, :])
        for tile in range(tiles):
            for side in range(2):
                left = side * half + tile * 128
                where = pl.ds(tile * 2 + side, width, stride=2 * tiles)
                piece = value[:, left : left + 128]
                grad_in_ref[where, :] = grad_in_ref[where, :] + piece if more else piece

    gather_z(0)
    gather_own(1)
    gather_own(0)
    gather_z(1)
    gather_own(2)
    gather_z(2)
    load_out.wait()
    w_out_t[...] = w_out_ref[...].T
    gather_plane(0)
    load_in.wait()
    w_in_t[...] = w_in_ref[...].T
    gather_plane(1)
    gather_far(0)
    gather_plane(2)
    gather_core(0)
    gather_far(1)
    gather_end(0)
    compute(0)
    gather_core(1)
    gather_far(2)
    scatter_plane(0)
    gather_end(1)
    compute(1)
    gather_core(2)
    scatter_near(0)
    scatter_plane(1)
    weight_out(0, 2, False)
    weight_in(0, 2, False)
    gather_end(2)
    compute(2)
    scatter_z(0)
    scatter_near(1)
    scatter_plane(2)
    weight_out(2, 3, True)
    save_out = pltpu.make_async_copy(grad_out_ref, grad_out_hbm, local_sem.at[1])
    save_out.start()
    scatter_near(2)
    scatter_z(1)
    weight_in(2, 3, True)
    save_in = pltpu.make_async_copy(grad_in_ref, grad_in_hbm, local_sem.at[0])
    save_in.start()
    scatter_z(2)
    last = len(sent) - 6
    for g in range(batches):
        if g == batches - 1:
            for copy in sent[:last]:
                copy.wait_send()
        scatter_end(g)
    total_mixed = jnp.concatenate(totals[0], axis=0)
    mixed_ref[...] = total_mixed[:, :width].astype(jnp.bfloat16)
    grad_tok_ref[...] = jnp.concatenate(totals[1], axis=0).astype(jnp.bfloat16)
    by_expert = total_mixed[:, width:]
    lines = []
    for k in range(per_token):
        chosen = jnp.logical_and(ids[k] == col_expert, col < 2 * groups)
        value = jnp.sum(jnp.where(chosen, by_expert, 0.0), axis=1, keepdims=True)
        lines.append(jnp.sum(jnp.where(diagonal, value, 0.0), axis=0, keepdims=True))
    grad_gates_ref[...] = jnp.concatenate(lines, axis=0)
    save_out.wait()
    save_in.wait()
    for copy in sent[last:]:
        copy.wait_send()


def dense_plan(tokens, grad_out, expert_ids, gates, w_in, w_out):
    count, width = tokens.shape
    groups = lax.axis_size("expert")
    half = w_out.shape[1]
    devices = 2 * groups
    batch = 8
    batches = count // batch
    vmem = pl.BlockSpec(memory_space=pltpu.VMEM)
    anywhere = pl.BlockSpec(memory_space=pl.ANY)
    total_rows = devices * count
    wide = width + GATE_COLS
    tiles = half // 128
    outs = pl.pallas_call(
        functools.partial(moe_kernel, groups),
        out_shape=(
            jax.ShapeDtypeStruct((count, width), jnp.bfloat16),
            jax.ShapeDtypeStruct((count, width), jnp.bfloat16),
            jax.ShapeDtypeStruct(gates.shape[::-1], jnp.float32),
            jax.ShapeDtypeStruct((width * 2 * tiles, 128), jnp.float32),
            jax.ShapeDtypeStruct((half, width), jnp.float32),
        ),
        in_specs=[vmem] * 4 + [anywhere] * 2,
        out_specs=[vmem] * 3 + [anywhere] * 2,
        scratch_shapes=[
            pltpu.VMEM((batches, devices, batch, wide), jnp.bfloat16),
            pltpu.VMEM((batches, devices, batch, width), jnp.bfloat16),
            pltpu.VMEM((batches, devices, batch, wide), jnp.bfloat16),
            pltpu.VMEM((batches, devices, batch, width), jnp.bfloat16),
            pltpu.VMEM((batches, devices, batch, wide), jnp.bfloat16),
            pltpu.VMEM((batches, devices, batch, width), jnp.bfloat16),
            pltpu.VMEM((total_rows, width), jnp.bfloat16),
            pltpu.VMEM((total_rows, width), jnp.bfloat16),
            pltpu.VMEM((total_rows, half), jnp.bfloat16),
            pltpu.VMEM((total_rows, 2 * half), jnp.bfloat16),
            pltpu.VMEM((width, 2 * half), jnp.bfloat16),
            pltpu.VMEM((half, width), jnp.bfloat16),
            pltpu.VMEM((2 * half, width), jnp.bfloat16),
            pltpu.VMEM((width, half), jnp.bfloat16),
            pltpu.VMEM((width * 2 * tiles, 128), jnp.float32),
            pltpu.VMEM((half, width), jnp.float32),
            pltpu.SemaphoreType.DMA((batches, 2, devices)),
            pltpu.SemaphoreType.DMA((batches, 2, devices)),
            pltpu.SemaphoreType.DMA((batches, 2, devices)),
            pltpu.SemaphoreType.DMA((batches, 2, devices)),
            pltpu.SemaphoreType.DMA((2,)),
        ],
        compiler_params=pltpu.CompilerParams(
            collective_id=0, has_side_effects=True, vmem_limit_bytes=44 * 1024 * 1024
        ),
        cost_estimate=pl.CostEstimate(
            flops=18 * total_rows * width * half,
            bytes_accessed=12 * width * half + 6 * width * half,
            transcendentals=total_rows * half,
        ),
    )(tokens, grad_out, expert_ids.T, gates.T, w_in.reshape(width, 2 * half), w_out[0])
    mixed, grad_tokens, grad_gates, grad_in, grad_out_w = outs
    grad_in = grad_in.reshape(width, tiles, 2, 128).transpose(0, 2, 1, 3).reshape(w_in.shape)
    return (mixed, grad_tokens, grad_gates.T, grad_in, grad_out_w[None])


def per_device(tokens, grad_out, expert_ids, gates, w_in, w_out):
    if lax.axis_size("expert") == 16 and lax.axis_size("dp") == 2:
        return dense_plan(tokens, grad_out, expert_ids, gates, w_in, w_out)
    return routed_plan(tokens, grad_out, expert_ids, gates, w_in, w_out)


def solution(mesh):
    in_specs = (
        P(("dp", "expert"), None),
        P(("dp", "expert"), None),
        P(("dp", "expert"), None),
        P(("dp", "expert"), None),
        P("expert", None, None, "dp"),
        P("expert", "dp", None),
    )
    out_specs = (
        P(("dp", "expert"), None),
        P(("dp", "expert"), None),
        P(("dp", "expert"), None),
        P("expert", None, None, "dp"),
        P("expert", "dp", None),
    )
    return jax.shard_map(
        per_device, mesh=mesh, in_specs=in_specs, out_specs=out_specs, check_vma=False
    )
```

```python
import functools

import jax
import jax.numpy as jnp
from jax import lax
from jax.experimental import pallas as pl
from jax.experimental.pallas import tpu as pltpu
from jax.sharding import PartitionSpec as P


def forward_part(rows, weight_in, weight_out):
    model_width = rows.shape[1]
    hidden_width = weight_out.shape[0]
    flat_in = weight_in.reshape(model_width, 2 * hidden_width)
    preact = jnp.dot(rows, flat_in, preferred_element_type=jnp.float32)
    gate_part = preact[:, :hidden_width]
    up_part = preact[:, hidden_width:]
    activated = gate_part * jax.nn.sigmoid(gate_part)
    hidden = (activated * up_part).astype(jnp.bfloat16)
    result = jnp.dot(hidden, weight_out, preferred_element_type=jnp.float32).astype(jnp.bfloat16)
    return (preact, hidden, result)


def backward_part(rows, preact, hidden, grad_rows, weight_in, weight_out):
    model_width = rows.shape[1]
    hidden_width = weight_out.shape[0]
    flat_in = weight_in.reshape(model_width, 2 * hidden_width)
    gate_part = preact[:, :hidden_width]
    up_part = preact[:, hidden_width:]
    sigmoid_gate = jax.nn.sigmoid(gate_part)
    activated = gate_part * sigmoid_gate
    back_grad = jnp.einsum("sd,hd->sh", grad_rows, weight_out, preferred_element_type=jnp.float32)
    grad_gate = back_grad * up_part * (sigmoid_gate * (1.0 + gate_part * (1.0 - sigmoid_gate)))
    grad_up = back_grad * activated
    grad_pre = jnp.concatenate([grad_gate, grad_up], axis=1).astype(jnp.bfloat16)
    grad_rows_in = jnp.einsum(
        "sk,dk->sd", grad_pre, flat_in, preferred_element_type=jnp.float32
    ).astype(jnp.bfloat16)
    grad_weight_in = jnp.einsum("sd,sk->dk", rows, grad_pre, preferred_element_type=jnp.float32)
    grad_weight_out = jnp.einsum("sh,sd->hd", hidden, grad_rows, preferred_element_type=jnp.float32)
    return (grad_rows_in, grad_weight_in, grad_weight_out)


def routed_plan(tokens, grad_out, expert_ids, gates, w_in, w_out):
    count_tok, model_width = tokens.shape
    per_token = expert_ids.shape[1]
    groups = lax.axis_size("expert")
    capacity = min(count_tok, 3 * count_tok * per_token // (2 * groups))
    row_count = count_tok * per_token
    flat_ids = expert_ids.reshape(-1)
    onehot = (flat_ids[:, None] == jnp.arange(groups, dtype=jnp.int32)[None, :]).astype(jnp.int32)
    order_rank = jnp.sum((jnp.cumsum(onehot, axis=0) - onehot) * onehot, axis=1)
    slot_of_row = flat_ids * capacity + order_rank
    inverse = (
        jnp.full((groups * capacity,), row_count, jnp.int32)
        .at[slot_of_row]
        .set(jnp.arange(row_count, dtype=jnp.int32))
    )
    token_of_slot = jnp.where(inverse < row_count, inverse // per_token, count_tok)
    tokens_padded = jnp.concatenate([tokens, jnp.zeros((1, model_width), jnp.bfloat16)], axis=0)
    grad_padded = jnp.concatenate([grad_out, jnp.zeros((1, model_width), jnp.bfloat16)], axis=0)
    gates_padded = jnp.concatenate([gates.reshape(-1), jnp.zeros((1,), jnp.float32)], axis=0)
    send_rows = tokens_padded[token_of_slot].reshape(groups, capacity, model_width)
    slot_gate = gates_padded[inverse]
    send_grads = (slot_gate[:, None] * grad_padded[token_of_slot].astype(jnp.float32)).astype(
        jnp.bfloat16
    )
    send_grads = send_grads.reshape(groups, capacity, model_width)
    full_in, full_out = (
        lax.all_gather(w_in, "dp", axis=3, tiled=True),
        lax.all_gather(w_out, "dp", axis=1, tiled=True),
    )
    weight_in = full_in[0]
    weight_out = full_out[0]
    hidden_width = weight_out.shape[0]
    arrived_rows = lax.all_to_all(send_rows, "expert", split_axis=0, concat_axis=0, tiled=True)
    rows = arrived_rows.reshape(groups * capacity, model_width)
    preact, hidden, result = forward_part(rows, weight_in, weight_out)
    back_out = lax.all_to_all(
        result.reshape(groups, capacity, model_width),
        "expert",
        split_axis=0,
        concat_axis=0,
        tiled=True,
    )
    arrived_grads = lax.all_to_all(send_grads, "expert", split_axis=0, concat_axis=0, tiled=True)
    grad_rows = arrived_grads.reshape(groups * capacity, model_width)
    grad_rows_in, grad_weight_in, grad_weight_out = backward_part(
        rows, preact, hidden, grad_rows, weight_in, weight_out
    )
    back_grads = lax.all_to_all(
        grad_rows_in.reshape(groups, capacity, model_width),
        "expert",
        split_axis=0,
        concat_axis=0,
        tiled=True,
    )
    out_rows = back_out.reshape(groups * capacity, model_width)[slot_of_row].reshape(
        count_tok, per_token, model_width
    )
    mixed = jnp.sum(gates[:, :, None] * out_rows.astype(jnp.float32), axis=1).astype(jnp.bfloat16)
    grad_gates = jnp.einsum("td,tkd->tk", grad_out, out_rows, preferred_element_type=jnp.float32)
    route_dx = back_grads.reshape(groups * capacity, model_width)[slot_of_row].reshape(
        count_tok, per_token, model_width
    )
    grad_tokens = jnp.sum(route_dx.astype(jnp.float32), axis=1).astype(jnp.bfloat16)
    grad_in_shard, grad_out_shard = (
        lax.psum_scatter(
            grad_weight_in.reshape(1, model_width, 2, hidden_width).astype(jnp.bfloat16),
            "dp",
            scatter_dimension=3,
            tiled=True,
        ).astype(jnp.float32),
        lax.psum_scatter(
            grad_weight_out[None].astype(jnp.bfloat16), "dp", scatter_dimension=1, tiled=True
        ).astype(jnp.float32),
    )
    return (mixed, grad_tokens, grad_gates, grad_in_shard, grad_out_shard)


MESH = pl.DeviceIdType.MESH
GATE_COLS = 128


def dot_tn(a, b):
    return lax.dot_general(a, b, (((0,), (0,)), ((), ())), preferred_element_type=jnp.float32)


def moe_kernel(
    groups, tokens_ref, cot_ref, ids_ref, gates_ref, w_in_hbm, w_out_hbm,
    mixed_ref, grad_tok_ref, grad_gates_ref, grad_in_hbm, grad_out_hbm,
    tok_all, cot_all, part_mixed, part_grad, recv_mixed, recv_grad,
    rows_buf, cot_buf, hidden_buf, pre_buf, w_in_ref, w_out_ref, w_in_t, w_out_t,
    grad_in_ref, grad_out_ref, their_in, their_out, give_in, give_out, take_in, take_out,
    gather_send, gather_recv, scatter_send, scatter_recv, local_sem, core_send, core_recv,
):
    count, width = tokens_ref.shape
    per_token = ids_ref.shape[0]
    half = w_out_ref.shape[1]
    batches, blocks, batch = tok_all.shape[:3]
    chunk = blocks * batch
    x = lax.axis_index("dp")
    e = lax.axis_index("expert")
    z, y, c = e // 4, (e // 2) % 2, e % 2

    def place(px, pz, py, pc):
        return (px, pz * 4 + py * 2 + pc)

    to_z = {
        1: place(x, z + 1 - 2 * (z % 2), y, c),
        2: place(x, (z + 2) % 4, y, c),
        3: place(x, 3 - z, y, c),
    }
    to_x = place(1 - x, z, y, c)
    to_y = place(x, z, 1 - y, c)
    to_core = place(x, z, y, 1 - c)

    partners = [to_z[1], to_z[2], to_z[3], to_x, to_y, to_core]
    barrier = pltpu.get_barrier_semaphore()
    for partner in partners:
        pl.semaphore_signal(barrier, inc=1, device_id=partner, device_id_type=MESH)
    load_in = pltpu.make_async_copy(w_in_hbm, w_in_ref.at[0], local_sem.at[0])
    load_out = pltpu.make_async_copy(w_out_hbm, w_out_ref.at[0], local_sem.at[1])
    load_in.start()
    load_out.start()

    col = lax.broadcasted_iota(jnp.int32, (count, GATE_COLS), 1)
    col_expert = (col % groups).astype(jnp.float32)
    diagonal = lax.broadcasted_iota(jnp.int32, (count, count), 0) == lax.broadcasted_iota(
        jnp.int32, (count, count), 1
    )
    ids_t = ids_ref[...].astype(jnp.float32)
    gates_t = gates_ref[...]

    def column(table, k):
        return jnp.sum(jnp.where(diagonal, table[k : k + 1, :], 0.0), axis=1, keepdims=True)

    ids = [column(ids_t, k) for k in range(per_token)]
    dense = jnp.zeros((count, GATE_COLS), jnp.float32)
    for k in range(per_token):
        dense = dense + jnp.where(ids[k] == col_expert, column(gates_t, k), 0.0)
    high = dense.astype(jnp.bfloat16).astype(jnp.float32)
    middle = (dense - high).astype(jnp.bfloat16).astype(jnp.float32)
    low = dense - high - middle
    pieces = jnp.where(
        col < groups,
        high,
        jnp.where(col < 2 * groups, middle, jnp.where(col < 3 * groups, low, 0.0)),
    )
    own_tokens = tokens_ref[...].astype(jnp.float32)
    own_cot = cot_ref[...].astype(jnp.float32)
    for g in range(batches):
        part = slice(g * batch, (g + 1) * batch)
        tok_all[g, 0, :, :width] = own_tokens[part].astype(jnp.bfloat16)
        tok_all[g, 0, :, width:] = pieces[part].astype(jnp.bfloat16)
        cot_all[g, 0] = own_cot[part].astype(jnp.bfloat16)
    pl.semaphore_wait(barrier, len(partners))

    def swap(src, dst, index):
        copy = pltpu.make_async_remote_copy(
            src_ref=src,
            dst_ref=dst,
            send_sem=core_send.at[index],
            recv_sem=core_recv.at[index],
            device_id=to_core,
            device_id_type=MESH,
        )
        copy.start()
        return copy

    swap_out = swap(w_out_hbm, w_out_ref.at[1], 0)
    swap_in = swap(w_in_hbm, w_in_ref.at[1], 1)

    gathered = (tok_all, cot_all)
    partial = (part_mixed, part_grad)
    landing = (recv_mixed, recv_grad)
    sent = []

    def copy_of(source, target, sems, g, h, src, dst, device, number):
        return pltpu.make_async_remote_copy(
            src_ref=source[h].at[g, pl.ds(src, number)],
            dst_ref=target[h].at[g, pl.ds(dst, number)],
            send_sem=sems[0].at[g, h, dst],
            recv_sem=sems[1].at[g, h, dst],
            device_id=device,
            device_id_type=MESH,
        )

    gather_sems = (gather_send, gather_recv)
    scatter_sems = (scatter_send, scatter_recv)

    def push(g, h, src, dst, device, number=4):
        copy = copy_of(gathered, gathered, gather_sems, g, h, src, dst, device, number)
        copy.start()
        sent.append(copy)

    def arrived(g, h, slot, number=4):
        copy_of(gathered, gathered, gather_sems, g, h, slot, slot, to_core, number).wait_recv()

    def give(g, h, src, dst, device, number=4):
        copy = copy_of(partial, landing, scatter_sems, g, h, src, dst, device, number)
        copy.start()
        sent.append(copy)

    def took(g, h, dst, number=4):
        copy_of(partial, landing, scatter_sems, g, h, 0, dst, to_core, number).wait_recv()

    def add(g, h, slot, dst, number=4):
        here = pl.ds(slot, number)
        partial[h][g, here] = (
            partial[h][g, here].astype(jnp.float32)
            + landing[h][g, pl.ds(dst, number)].astype(jnp.float32)
        ).astype(jnp.bfloat16)

    first = (to_x, to_y)
    second = (to_y, to_x)
    first_slot = (8, 4)
    second_slot = (4, 8)

    plane_first = [g == 1 for g in range(batches)]

    def gather_z(g):
        for dz in (1, 3, 2):
            for h in (0, 1):
                push(g, h, 0, dz, to_z[dz], 1)

    def gather_own(g):
        for h in (0, 1):
            push(g, h, 0, first_slot[h], first[h], 1)
        if not plane_first[g]:
            for h in (0, 1):
                push(g, h, 0, second_slot[h], second[h], 1)

    def gather_plane(g):
        if plane_first[g]:
            for h in (0, 1):
                slot = first_slot[h]
                arrived(g, h, slot, 1)
                for dz in (1, 3, 2):
                    push(g, h, slot, slot + dz, to_z[dz], 1)
        for h in (0, 1):
            for dz in (1, 3, 2):
                arrived(g, h, dz, 1)
            if plane_first[g]:
                push(g, h, 0, second_slot[h], second[h])
            else:
                push(g, h, 1, first_slot[h] + 1, first[h], 3)
                push(g, h, 1, second_slot[h] + 1, second[h], 3)

    def gather_far(g):
        for h in (0, 1):
            slot = first_slot[h]
            if plane_first[g]:
                for dz in (1, 3, 2):
                    arrived(g, h, slot + dz, 1)
            else:
                arrived(g, h, slot, 1)
                arrived(g, h, slot + 1, 3)
            push(g, h, slot, 12, second[h])

    def gather_end(g):
        for h in (0, 1):
            slot = second_slot[h]
            if plane_first[g]:
                arrived(g, h, slot)
            else:
                arrived(g, h, slot, 1)
                arrived(g, h, slot + 1, 3)
            arrived(g, h, 12)

    wide_col = lax.broadcasted_iota(jnp.int32, (chunk, GATE_COLS), 1)

    def compute(g):
        here = pl.ds(chunk * g, chunk)
        packed = tok_all[g].astype(jnp.float32).reshape(chunk, width + GATE_COLS)
        rows = packed[:, :width].astype(jnp.bfloat16)
        cot = cot_all[g].astype(jnp.float32).reshape(chunk, width).astype(jnp.bfloat16)
        rows_buf[here, :] = rows
        cot_buf[here, :] = cot
        mixed = jnp.zeros((chunk, width), jnp.float32)
        grad_rows = jnp.zeros((chunk, width), jnp.float32)
        spread = jnp.zeros((chunk, GATE_COLS), jnp.float32)
        for side, expert in ((0, e), (1, e + 1 - 2 * c)):
            own = jnp.logical_and(wide_col % groups == expert, wide_col < 3 * groups)
            gate = jnp.sum(jnp.where(own, packed[:, width:], 0.0), axis=1, keepdims=True)
            preact = jnp.dot(rows, w_in_ref[side], preferred_element_type=jnp.float32)
            gate_part = preact[:, :half]
            up_part = preact[:, half:]
            sig = jax.nn.sigmoid(gate_part)
            activated = gate_part * sig
            hidden = activated * up_part
            back = jnp.dot(cot, w_out_t[side], preferred_element_type=jnp.float32)
            gate_grad = jnp.sum(hidden * back, axis=1, keepdims=True)
            gated_hidden = (gate * hidden).astype(jnp.bfloat16)
            gated_back = gate * back
            grad_gate = gated_back * up_part * (sig * (1.0 + gate_part * (1.0 - sig)))
            grad_up = gated_back * activated
            grad_pre = jnp.concatenate([grad_gate, grad_up], axis=1).astype(jnp.bfloat16)
            hidden_buf[side, here, :] = gated_hidden
            pre_buf[side, here, :] = grad_pre
            mixed = mixed + jnp.dot(
                gated_hidden, w_out_ref[side], preferred_element_type=jnp.float32
            )
            grad_rows = grad_rows + jnp.dot(
                grad_pre, w_in_t[side], preferred_element_type=jnp.float32
            )
            high = gate_grad.astype(jnp.bfloat16).astype(jnp.float32)
            spread = spread + jnp.where(
                wide_col == expert,
                high,
                jnp.where(wide_col == groups + expert, gate_grad - high, 0.0),
            )
        part_mixed[g, :, :, :width] = mixed.reshape(blocks, batch, width).astype(jnp.bfloat16)
        part_mixed[g, :, :, width:] = spread.reshape(blocks, batch, GATE_COLS).astype(
            jnp.bfloat16
        )
        part_grad[g] = grad_rows.reshape(blocks, batch, width).astype(jnp.bfloat16)

    def scatter_plane(g):
        for h in (0, 1):
            give(g, h, 12, 20, second[h])
        for h in (0, 1):
            give(g, h, second_slot[h], 16, second[h])

    def scatter_near(g):
        for h in (0, 1):
            slot = first_slot[h]
            took(g, h, 20)
            add(g, h, slot, 20)
            if plane_first[g]:
                for dz in (2, 3, 1):
                    give(g, h, slot + dz, 24 + dz, to_z[dz], 1)
            else:
                give(g, h, slot, 24, first[h])

    def scatter_z(g):
        for h in (0, 1):
            took(g, h, 16)
            add(g, h, 0, 16)
            if plane_first[g]:
                for dz in (2, 3, 1):
                    give(g, h, dz, 28 + dz, to_z[dz], 1)
        for h in (0, 1):
            if plane_first[g]:
                slot = first_slot[h]
                for dz in (1, 3, 2):
                    took(g, h, 24 + dz, 1)
                total = partial[h][g, slot].astype(jnp.float32)
                for dz in (1, 3, 2):
                    total = total + landing[h][g, 24 + dz].astype(jnp.float32)
                partial[h][g, slot] = total.astype(jnp.bfloat16)
                give(g, h, slot, 24, first[h], 1)
            else:
                took(g, h, 24)
                add(g, h, 0, 24)
                for dz in (2, 3, 1):
                    give(g, h, dz, 28 + dz, to_z[dz], 1)

    totals = ([], [])

    def scatter_end(g):
        for h in (0, 1):
            total = partial[h][g, 0].astype(jnp.float32)
            for dz in (1, 3, 2):
                took(g, h, 28 + dz, 1)
                total = total + landing[h][g, 28 + dz].astype(jnp.float32)
            if plane_first[g]:
                took(g, h, 24, 1)
                total = total + landing[h][g, 24].astype(jnp.float32)
            totals[h].append(total)

    tiles = half // 128

    def weight_out(lower, upper, more):
        part = pl.ds(lower * chunk, (upper - lower) * chunk)
        value = dot_tn(hidden_buf[0, part, :], cot_buf[part, :])
        grad_out_ref[...] = grad_out_ref[...] + value if more else value

    def weight_in(lower, upper, more):
        part = pl.ds(lower * chunk, (upper - lower) * chunk)
        value = dot_tn(rows_buf[part, :], pre_buf[0, part, :])
        for tile in range(tiles):
            for side in range(2):
                left = side * half + tile * 128
                where = pl.ds(tile * 2 + side, width, stride=2 * tiles)
                piece = value[:, left : left + 128]
                grad_in_ref[where, :] = grad_in_ref[where, :] + piece if more else piece

    def their_weights(lower, upper, more):
        part = pl.ds(lower * chunk, (upper - lower) * chunk)
        value = dot_tn(hidden_buf[1, part, :], cot_buf[part, :])
        if more:
            give_out[...] = (their_out[...] + value).astype(jnp.bfloat16)
            swaps.append(swap(give_out, take_out, 2))
        else:
            their_out[...] = value
        value = dot_tn(rows_buf[part, :], pre_buf[1, part, :])
        if more:
            give_in[...] = (their_in[...] + value).astype(jnp.bfloat16)
            swaps.append(swap(give_in, take_in, 3))
        else:
            their_in[...] = value

    swaps = [swap_out, swap_in]

    gather_z(0)
    gather_own(1)
    gather_own(0)
    gather_z(1)
    gather_own(2)
    gather_z(2)
    load_out.wait()
    w_out_t[0] = w_out_ref[0].T
    gather_plane(0)
    load_in.wait()
    w_in_t[0] = w_in_ref[0].T
    gather_plane(1)
    gather_far(0)
    gather_plane(2)
    swap_out.wait_recv()
    w_out_t[1] = w_out_ref[1].T
    swap_in.wait_recv()
    w_in_t[1] = w_in_ref[1].T
    gather_far(1)
    gather_end(0)
    compute(0)
    scatter_plane(0)
    gather_far(2)
    gather_end(1)
    compute(1)
    scatter_plane(1)
    scatter_near(0)
    their_weights(0, 2, False)
    weight_out(0, 2, False)
    weight_in(0, 2, False)
    gather_end(2)
    compute(2)
    scatter_plane(2)
    scatter_z(0)
    scatter_near(1)
    their_weights(2, 3, True)
    scatter_near(2)
    scatter_z(1)
    weight_out(2, 3, True)
    weight_in(2, 3, True)
    scatter_z(2)
    swaps[2].wait_recv()
    grad_out_ref[...] = grad_out_ref[...] + take_out[...].astype(jnp.float32)
    save_out = pltpu.make_async_copy(grad_out_ref, grad_out_hbm, local_sem.at[1])
    save_out.start()
    swaps[3].wait_recv()
    for tile in range(tiles):
        for side in range(2):
            left = side * half + tile * 128
            where = pl.ds(tile * 2 + side, width, stride=2 * tiles)
            grad_in_ref[where, :] = grad_in_ref[where, :] + take_in[
                :, left : left + 128
            ].astype(jnp.float32)
    save_in = pltpu.make_async_copy(grad_in_ref, grad_in_hbm, local_sem.at[0])
    save_in.start()
    last = len(sent) - 6
    for g in range(batches):
        if g == batches - 1:
            for copy in sent[:last]:
                copy.wait_send()
        scatter_end(g)
    total_mixed = jnp.concatenate(totals[0], axis=0)
    mixed_ref[...] = total_mixed[:, :width].astype(jnp.bfloat16)
    grad_tok_ref[...] = jnp.concatenate(totals[1], axis=0).astype(jnp.bfloat16)
    by_expert = total_mixed[:, width:]
    lines = []
    for k in range(per_token):
        chosen = jnp.logical_and(ids[k] == col_expert, col < 2 * groups)
        value = jnp.sum(jnp.where(chosen, by_expert, 0.0), axis=1, keepdims=True)
        lines.append(jnp.sum(jnp.where(diagonal, value, 0.0), axis=0, keepdims=True))
    grad_gates_ref[...] = jnp.concatenate(lines, axis=0)
    save_out.wait()
    save_in.wait()
    for copy in swaps + sent[last:]:
        copy.wait_send()


def dense_plan(tokens, grad_out, expert_ids, gates, w_in, w_out):
    count, width = tokens.shape
    groups = lax.axis_size("expert")
    half = w_out.shape[1]
    devices = 2 * groups
    batch = 8
    batches = count // batch
    vmem = pl.BlockSpec(memory_space=pltpu.VMEM)
    anywhere = pl.BlockSpec(memory_space=pl.ANY)
    total_rows = devices * count
    wide = width + GATE_COLS
    tiles = half // 128
    outs = pl.pallas_call(
        functools.partial(moe_kernel, groups),
        out_shape=(
            jax.ShapeDtypeStruct((count, width), jnp.bfloat16),
            jax.ShapeDtypeStruct((count, width), jnp.bfloat16),
            jax.ShapeDtypeStruct(gates.shape[::-1], jnp.float32),
            jax.ShapeDtypeStruct((width * 2 * tiles, 128), jnp.float32),
            jax.ShapeDtypeStruct((half, width), jnp.float32),
        ),
        in_specs=[vmem] * 4 + [anywhere] * 2,
        out_specs=[vmem] * 3 + [anywhere] * 2,
        scratch_shapes=[
            pltpu.VMEM((batches, groups, batch, wide), jnp.bfloat16),
            pltpu.VMEM((batches, groups, batch, width), jnp.bfloat16),
            pltpu.VMEM((batches, groups, batch, wide), jnp.bfloat16),
            pltpu.VMEM((batches, groups, batch, width), jnp.bfloat16),
            pltpu.VMEM((batches, devices, batch, wide), jnp.bfloat16),
            pltpu.VMEM((batches, devices, batch, width), jnp.bfloat16),
            pltpu.VMEM((total_rows // 2, width), jnp.bfloat16),
            pltpu.VMEM((total_rows // 2, width), jnp.bfloat16),
            pltpu.VMEM((2, total_rows // 2, half), jnp.bfloat16),
            pltpu.VMEM((2, total_rows // 2, 2 * half), jnp.bfloat16),
            pltpu.VMEM((2, width, 2 * half), jnp.bfloat16),
            pltpu.VMEM((2, half, width), jnp.bfloat16),
            pltpu.VMEM((2, 2 * half, width), jnp.bfloat16),
            pltpu.VMEM((2, width, half), jnp.bfloat16),
            pltpu.VMEM((width * 2 * tiles, 128), jnp.float32),
            pltpu.VMEM((half, width), jnp.float32),
            pltpu.VMEM((width, 2 * half), jnp.float32),
            pltpu.VMEM((half, width), jnp.float32),
            pltpu.VMEM((width, 2 * half), jnp.bfloat16),
            pltpu.VMEM((half, width), jnp.bfloat16),
            pltpu.VMEM((width, 2 * half), jnp.bfloat16),
            pltpu.VMEM((half, width), jnp.bfloat16),
            pltpu.SemaphoreType.DMA((batches, 2, devices)),
            pltpu.SemaphoreType.DMA((batches, 2, devices)),
            pltpu.SemaphoreType.DMA((batches, 2, devices)),
            pltpu.SemaphoreType.DMA((batches, 2, devices)),
            pltpu.SemaphoreType.DMA((2,)),
            pltpu.SemaphoreType.DMA((4,)),
            pltpu.SemaphoreType.DMA((4,)),
        ],
        compiler_params=pltpu.CompilerParams(
            collective_id=0, has_side_effects=True, vmem_limit_bytes=44 * 1024 * 1024
        ),
        cost_estimate=pl.CostEstimate(
            flops=18 * total_rows * width * half,
            bytes_accessed=12 * width * half + 6 * width * half,
            transcendentals=total_rows * half,
        ),
    )(tokens, grad_out, expert_ids.T, gates.T, w_in.reshape(width, 2 * half), w_out[0])
    mixed, grad_tokens, grad_gates, grad_in, grad_out_w = outs
    grad_in = grad_in.reshape(width, tiles, 2, 128).transpose(0, 2, 1, 3).reshape(w_in.shape)
    return (mixed, grad_tokens, grad_gates.T, grad_in, grad_out_w[None])


def per_device(tokens, grad_out, expert_ids, gates, w_in, w_out):
    if lax.axis_size("expert") == 16 and lax.axis_size("dp") == 2:
        return dense_plan(tokens, grad_out, expert_ids, gates, w_in, w_out)
    return routed_plan(tokens, grad_out, expert_ids, gates, w_in, w_out)


def solution(mesh):
    in_specs = (
        P(("dp", "expert"), None),
        P(("dp", "expert"), None),
        P(("dp", "expert"), None),
        P(("dp", "expert"), None),
        P("expert", None, None, "dp"),
        P("expert", "dp", None),
    )
    out_specs = (
        P(("dp", "expert"), None),
        P(("dp", "expert"), None),
        P(("dp", "expert"), None),
        P("expert", None, None, "dp"),
        P("expert", "dp", None),
    )
    return jax.shard_map(
        per_device, mesh=mesh, in_specs=in_specs, out_specs=out_specs, check_vma=False
    )
```

```python
import functools

import jax
import jax.numpy as jnp
from jax import lax
from jax.experimental import pallas as pl
from jax.experimental.pallas import tpu as pltpu
from jax.sharding import PartitionSpec as P


def forward_part(rows, weight_in, weight_out):
    model_width = rows.shape[1]
    hidden_width = weight_out.shape[0]
    flat_in = weight_in.reshape(model_width, 2 * hidden_width)
    preact = jnp.dot(rows, flat_in, preferred_element_type=jnp.float32)
    gate_part = preact[:, :hidden_width]
    up_part = preact[:, hidden_width:]
    activated = gate_part * jax.nn.sigmoid(gate_part)
    hidden = (activated * up_part).astype(jnp.bfloat16)
    result = jnp.dot(hidden, weight_out, preferred_element_type=jnp.float32).astype(jnp.bfloat16)
    return (preact, hidden, result)


def backward_part(rows, preact, hidden, grad_rows, weight_in, weight_out):
    model_width = rows.shape[1]
    hidden_width = weight_out.shape[0]
    flat_in = weight_in.reshape(model_width, 2 * hidden_width)
    gate_part = preact[:, :hidden_width]
    up_part = preact[:, hidden_width:]
    sigmoid_gate = jax.nn.sigmoid(gate_part)
    activated = gate_part * sigmoid_gate
    back_grad = jnp.einsum("sd,hd->sh", grad_rows, weight_out, preferred_element_type=jnp.float32)
    grad_gate = back_grad * up_part * (sigmoid_gate * (1.0 + gate_part * (1.0 - sigmoid_gate)))
    grad_up = back_grad * activated
    grad_pre = jnp.concatenate([grad_gate, grad_up], axis=1).astype(jnp.bfloat16)
    grad_rows_in = jnp.einsum(
        "sk,dk->sd", grad_pre, flat_in, preferred_element_type=jnp.float32
    ).astype(jnp.bfloat16)
    grad_weight_in = jnp.einsum("sd,sk->dk", rows, grad_pre, preferred_element_type=jnp.float32)
    grad_weight_out = jnp.einsum("sh,sd->hd", hidden, grad_rows, preferred_element_type=jnp.float32)
    return (grad_rows_in, grad_weight_in, grad_weight_out)


def routed_plan(tokens, grad_out, expert_ids, gates, w_in, w_out):
    count_tok, model_width = tokens.shape
    per_token = expert_ids.shape[1]
    groups = lax.axis_size("expert")
    capacity = min(count_tok, 3 * count_tok * per_token // (2 * groups))
    row_count = count_tok * per_token
    flat_ids = expert_ids.reshape(-1)
    onehot = (flat_ids[:, None] == jnp.arange(groups, dtype=jnp.int32)[None, :]).astype(jnp.int32)
    order_rank = jnp.sum((jnp.cumsum(onehot, axis=0) - onehot) * onehot, axis=1)
    slot_of_row = flat_ids * capacity + order_rank
    inverse = (
        jnp.full((groups * capacity,), row_count, jnp.int32)
        .at[slot_of_row]
        .set(jnp.arange(row_count, dtype=jnp.int32))
    )
    token_of_slot = jnp.where(inverse < row_count, inverse // per_token, count_tok)
    tokens_padded = jnp.concatenate([tokens, jnp.zeros((1, model_width), jnp.bfloat16)], axis=0)
    grad_padded = jnp.concatenate([grad_out, jnp.zeros((1, model_width), jnp.bfloat16)], axis=0)
    gates_padded = jnp.concatenate([gates.reshape(-1), jnp.zeros((1,), jnp.float32)], axis=0)
    send_rows = tokens_padded[token_of_slot].reshape(groups, capacity, model_width)
    slot_gate = gates_padded[inverse]
    send_grads = (slot_gate[:, None] * grad_padded[token_of_slot].astype(jnp.float32)).astype(
        jnp.bfloat16
    )
    send_grads = send_grads.reshape(groups, capacity, model_width)
    full_in, full_out = (
        lax.all_gather(w_in, "dp", axis=3, tiled=True),
        lax.all_gather(w_out, "dp", axis=1, tiled=True),
    )
    weight_in = full_in[0]
    weight_out = full_out[0]
    hidden_width = weight_out.shape[0]
    arrived_rows = lax.all_to_all(send_rows, "expert", split_axis=0, concat_axis=0, tiled=True)
    rows = arrived_rows.reshape(groups * capacity, model_width)
    preact, hidden, result = forward_part(rows, weight_in, weight_out)
    back_out = lax.all_to_all(
        result.reshape(groups, capacity, model_width),
        "expert",
        split_axis=0,
        concat_axis=0,
        tiled=True,
    )
    arrived_grads = lax.all_to_all(send_grads, "expert", split_axis=0, concat_axis=0, tiled=True)
    grad_rows = arrived_grads.reshape(groups * capacity, model_width)
    grad_rows_in, grad_weight_in, grad_weight_out = backward_part(
        rows, preact, hidden, grad_rows, weight_in, weight_out
    )
    back_grads = lax.all_to_all(
        grad_rows_in.reshape(groups, capacity, model_width),
        "expert",
        split_axis=0,
        concat_axis=0,
        tiled=True,
    )
    out_rows = back_out.reshape(groups * capacity, model_width)[slot_of_row].reshape(
        count_tok, per_token, model_width
    )
    mixed = jnp.sum(gates[:, :, None] * out_rows.astype(jnp.float32), axis=1).astype(jnp.bfloat16)
    grad_gates = jnp.einsum("td,tkd->tk", grad_out, out_rows, preferred_element_type=jnp.float32)
    route_dx = back_grads.reshape(groups * capacity, model_width)[slot_of_row].reshape(
        count_tok, per_token, model_width
    )
    grad_tokens = jnp.sum(route_dx.astype(jnp.float32), axis=1).astype(jnp.bfloat16)
    grad_in_shard, grad_out_shard = (
        lax.psum_scatter(
            grad_weight_in.reshape(1, model_width, 2, hidden_width).astype(jnp.bfloat16),
            "dp",
            scatter_dimension=3,
            tiled=True,
        ).astype(jnp.float32),
        lax.psum_scatter(
            grad_weight_out[None].astype(jnp.bfloat16), "dp", scatter_dimension=1, tiled=True
        ).astype(jnp.float32),
    )
    return (mixed, grad_tokens, grad_gates, grad_in_shard, grad_out_shard)


MESH = pl.DeviceIdType.MESH
GATE_COLS = 128


def dot_tn(a, b):
    return lax.dot_general(a, b, (((0,), (0,)), ((), ())), preferred_element_type=jnp.float32)


def moe_kernel(
    groups, tokens_ref, cot_ref, ids_ref, gates_ref, w_in_hbm, w_out_hbm,
    mixed_ref, grad_tok_ref, grad_gates_ref, grad_in_ref, grad_out_ref,
    tok_all, cot_all, part_mixed, part_grad, recv_mixed, recv_grad,
    rows_buf, cot_buf, hidden_buf, pre_buf, w_in_ref, w_out_ref, w_in_t, w_out_t,
    give_in, give_out, take_in, take_out,
    gather_send, gather_recv, scatter_send, scatter_recv, local_sem, core_send, core_recv,
):
    count, width = tokens_ref.shape
    per_token = ids_ref.shape[0]
    half = w_out_ref.shape[1]
    batches, blocks, batch = tok_all.shape[:3]
    chunk = blocks * batch
    x = lax.axis_index("dp")
    e = lax.axis_index("expert")
    z, y, c = e // 4, (e // 2) % 2, e % 2

    def place(px, pz, py, pc):
        return (px, pz * 4 + py * 2 + pc)

    to_z = {
        1: place(x, z + 1 - 2 * (z % 2), y, c),
        2: place(x, (z + 2) % 4, y, c),
        3: place(x, 3 - z, y, c),
    }
    to_x = place(1 - x, z, y, c)
    to_y = place(x, z, 1 - y, c)
    to_core = place(x, z, y, 1 - c)

    partners = [to_z[1], to_z[2], to_z[3], to_x, to_y, to_core]
    barrier = pltpu.get_barrier_semaphore()
    for partner in partners:
        pl.semaphore_signal(barrier, inc=1, device_id=partner, device_id_type=MESH)
    load_in = pltpu.make_async_copy(w_in_hbm, w_in_ref.at[0], local_sem.at[0])
    load_out = pltpu.make_async_copy(w_out_hbm, w_out_ref.at[0], local_sem.at[1])
    load_in.start()
    load_out.start()

    col = lax.broadcasted_iota(jnp.int32, (count, GATE_COLS), 1)
    col_expert = (col % groups).astype(jnp.float32)
    diagonal = lax.broadcasted_iota(jnp.int32, (count, count), 0) == lax.broadcasted_iota(
        jnp.int32, (count, count), 1
    )
    ids_t = ids_ref[...].astype(jnp.float32)
    gates_t = gates_ref[...]

    def column(table, k):
        return jnp.sum(jnp.where(diagonal, table[k : k + 1, :], 0.0), axis=1, keepdims=True)

    ids = [column(ids_t, k) for k in range(per_token)]
    dense = jnp.zeros((count, GATE_COLS), jnp.float32)
    for k in range(per_token):
        dense = dense + jnp.where(ids[k] == col_expert, column(gates_t, k), 0.0)
    high = dense.astype(jnp.bfloat16).astype(jnp.float32)
    middle = (dense - high).astype(jnp.bfloat16).astype(jnp.float32)
    low = dense - high - middle
    pieces = jnp.where(
        col < groups,
        high,
        jnp.where(col < 2 * groups, middle, jnp.where(col < 3 * groups, low, 0.0)),
    )
    own_tokens = tokens_ref[...].astype(jnp.float32)
    own_cot = cot_ref[...].astype(jnp.float32)
    for g in range(batches):
        part = slice(g * batch, (g + 1) * batch)
        tok_all[g, 0, :, :width] = own_tokens[part].astype(jnp.bfloat16)
        tok_all[g, 0, :, width:] = pieces[part].astype(jnp.bfloat16)
        cot_all[g, 0] = own_cot[part].astype(jnp.bfloat16)
    pl.semaphore_wait(barrier, len(partners))

    def swap(src, dst, index):
        copy = pltpu.make_async_remote_copy(
            src_ref=src,
            dst_ref=dst,
            send_sem=core_send.at[index],
            recv_sem=core_recv.at[index],
            device_id=to_core,
            device_id_type=MESH,
        )
        copy.start()
        return copy

    swap_out = swap(w_out_hbm, w_out_ref.at[1], 0)
    swap_in = swap(w_in_hbm, w_in_ref.at[1], 1)

    gathered = (tok_all, cot_all)
    partial = (part_mixed, part_grad)
    landing = (recv_mixed, recv_grad)
    sent = []

    def copy_of(source, target, sems, g, h, src, dst, device, number):
        return pltpu.make_async_remote_copy(
            src_ref=source[h].at[g, pl.ds(src, number)],
            dst_ref=target[h].at[g, pl.ds(dst, number)],
            send_sem=sems[0].at[g, h, dst],
            recv_sem=sems[1].at[g, h, dst],
            device_id=device,
            device_id_type=MESH,
        )

    gather_sems = (gather_send, gather_recv)
    scatter_sems = (scatter_send, scatter_recv)

    def push(g, h, src, dst, device, number=4):
        copy = copy_of(gathered, gathered, gather_sems, g, h, src, dst, device, number)
        copy.start()
        sent.append(copy)

    def arrived(g, h, slot, number=4):
        copy_of(gathered, gathered, gather_sems, g, h, slot, slot, to_core, number).wait_recv()

    def give(g, h, src, dst, device, number=4):
        copy = copy_of(partial, landing, scatter_sems, g, h, src, dst, device, number)
        copy.start()
        sent.append(copy)

    def took(g, h, dst, number=4):
        copy_of(partial, landing, scatter_sems, g, h, 0, dst, to_core, number).wait_recv()

    def add(g, h, slot, dst, number=4):
        here = pl.ds(slot, number)
        partial[h][g, here] = (
            partial[h][g, here].astype(jnp.float32)
            + landing[h][g, pl.ds(dst, number)].astype(jnp.float32)
        ).astype(jnp.bfloat16)

    first = (to_x, to_y)
    second = (to_y, to_x)
    first_slot = (8, 4)
    second_slot = (4, 8)

    plane_first = [g == 1 for g in range(batches)]

    def gather_z(g):
        for dz in (1, 3, 2):
            for h in (0, 1):
                push(g, h, 0, dz, to_z[dz], 1)

    def gather_own(g):
        for h in (0, 1):
            push(g, h, 0, first_slot[h], first[h], 1)
        if not plane_first[g]:
            for h in (0, 1):
                push(g, h, 0, second_slot[h], second[h], 1)

    def gather_plane(g):
        if plane_first[g]:
            for h in (0, 1):
                slot = first_slot[h]
                arrived(g, h, slot, 1)
                for dz in (1, 3, 2):
                    push(g, h, slot, slot + dz, to_z[dz], 1)
        for h in (0, 1):
            for dz in (1, 3, 2):
                arrived(g, h, dz, 1)
            if plane_first[g]:
                push(g, h, 0, second_slot[h], second[h])
            else:
                push(g, h, 1, first_slot[h] + 1, first[h], 3)
                push(g, h, 1, second_slot[h] + 1, second[h], 3)

    def gather_far(g):
        for h in (0, 1):
            slot = first_slot[h]
            if plane_first[g]:
                for dz in (1, 3, 2):
                    arrived(g, h, slot + dz, 1)
            else:
                arrived(g, h, slot, 1)
                arrived(g, h, slot + 1, 3)
            push(g, h, slot, 12, second[h])

    def gather_end(g):
        for h in (0, 1):
            slot = second_slot[h]
            if plane_first[g]:
                arrived(g, h, slot)
            else:
                arrived(g, h, slot, 1)
                arrived(g, h, slot + 1, 3)
            arrived(g, h, 12)

    wide_col = lax.broadcasted_iota(jnp.int32, (chunk, GATE_COLS), 1)

    def compute(g):
        here = pl.ds(chunk * g, chunk)
        packed = tok_all[g].astype(jnp.float32).reshape(chunk, width + GATE_COLS)
        rows = packed[:, :width].astype(jnp.bfloat16)
        cot = cot_all[g].astype(jnp.float32).reshape(chunk, width).astype(jnp.bfloat16)
        rows_buf[here, :] = rows
        cot_buf[here, :] = cot
        mixed = jnp.zeros((chunk, width), jnp.float32)
        grad_rows = jnp.zeros((chunk, width), jnp.float32)
        spread = jnp.zeros((chunk, GATE_COLS), jnp.float32)
        for side, expert in ((0, e), (1, e + 1 - 2 * c)):
            own = jnp.logical_and(wide_col % groups == expert, wide_col < 3 * groups)
            gate = jnp.sum(jnp.where(own, packed[:, width:], 0.0), axis=1, keepdims=True)
            preact = jnp.dot(rows, w_in_ref[side], preferred_element_type=jnp.float32)
            gate_part = preact[:, :half]
            up_part = preact[:, half:]
            sig = jax.nn.sigmoid(gate_part)
            activated = gate_part * sig
            hidden = activated * up_part
            back = jnp.dot(cot, w_out_t[side], preferred_element_type=jnp.float32)
            gate_grad = jnp.sum(hidden * back, axis=1, keepdims=True)
            gated_hidden = (gate * hidden).astype(jnp.bfloat16)
            gated_back = gate * back
            grad_gate = gated_back * up_part * (sig * (1.0 + gate_part * (1.0 - sig)))
            grad_up = gated_back * activated
            grad_pre = jnp.concatenate([grad_gate, grad_up], axis=1).astype(jnp.bfloat16)
            hidden_buf[side, here, :] = gated_hidden
            pre_buf[side, here, :] = grad_pre
            mixed = mixed + jnp.dot(
                gated_hidden, w_out_ref[side], preferred_element_type=jnp.float32
            )
            grad_rows = grad_rows + jnp.dot(
                grad_pre, w_in_t[side], preferred_element_type=jnp.float32
            )
            high = gate_grad.astype(jnp.bfloat16).astype(jnp.float32)
            spread = spread + jnp.where(
                wide_col == expert,
                high,
                jnp.where(wide_col == groups + expert, gate_grad - high, 0.0),
            )
        part_mixed[g, :, :, :width] = mixed.reshape(blocks, batch, width).astype(jnp.bfloat16)
        part_mixed[g, :, :, width:] = spread.reshape(blocks, batch, GATE_COLS).astype(
            jnp.bfloat16
        )
        part_grad[g] = grad_rows.reshape(blocks, batch, width).astype(jnp.bfloat16)

    def scatter_plane(g):
        for h in (0, 1):
            give(g, h, 12, 20, second[h])
        for h in (0, 1):
            give(g, h, second_slot[h], 16, second[h])

    def scatter_near(g):
        for h in (0, 1):
            slot = first_slot[h]
            took(g, h, 20)
            add(g, h, slot, 20)
            if plane_first[g]:
                for dz in (2, 3, 1):
                    give(g, h, slot + dz, 24 + dz, to_z[dz], 1)
            else:
                give(g, h, slot, 24, first[h])

    def scatter_z(g):
        for h in (0, 1):
            took(g, h, 16)
            add(g, h, 0, 16)
            if plane_first[g]:
                for dz in (2, 3, 1):
                    give(g, h, dz, 28 + dz, to_z[dz], 1)
        for h in (0, 1):
            if plane_first[g]:
                slot = first_slot[h]
                for dz in (1, 3, 2):
                    took(g, h, 24 + dz, 1)
                total = partial[h][g, slot].astype(jnp.float32)
                for dz in (1, 3, 2):
                    total = total + landing[h][g, 24 + dz].astype(jnp.float32)
                partial[h][g, slot] = total.astype(jnp.bfloat16)
                give(g, h, slot, 24, first[h], 1)
            else:
                took(g, h, 24)
                add(g, h, 0, 24)
                for dz in (2, 3, 1):
                    give(g, h, dz, 28 + dz, to_z[dz], 1)

    totals = ([], [])

    def scatter_end(g):
        for h in (0, 1):
            total = partial[h][g, 0].astype(jnp.float32)
            for dz in (1, 3, 2):
                took(g, h, 28 + dz, 1)
                total = total + landing[h][g, 28 + dz].astype(jnp.float32)
            if plane_first[g]:
                took(g, h, 24, 1)
                total = total + landing[h][g, 24].astype(jnp.float32)
            totals[h].append(total)

    tiles = half // 128

    def own_weights():
        grad_out_ref[...] = dot_tn(hidden_buf[0], cot_buf[...])
        value = dot_tn(rows_buf[...], pre_buf[0])
        for tile in range(tiles):
            for side in range(2):
                left = side * half + tile * 128
                where = pl.ds(tile * 2 + side, width, stride=2 * tiles)
                grad_in_ref[where, :] = value[:, left : left + 128]

    def their_weights():
        give_in[...] = dot_tn(rows_buf[...], pre_buf[1]).astype(jnp.bfloat16)
        swaps.append(swap(give_in, take_in, 3))
        give_out[...] = dot_tn(hidden_buf[1], cot_buf[...]).astype(jnp.bfloat16)
        swaps.append(swap(give_out, take_out, 2))

    swaps = [swap_out, swap_in]

    gather_z(0)
    gather_own(1)
    gather_own(0)
    gather_z(1)
    gather_own(2)
    gather_z(2)
    load_out.wait()
    w_out_t[0] = w_out_ref[0].T
    gather_plane(0)
    load_in.wait()
    w_in_t[0] = w_in_ref[0].T
    gather_plane(1)
    gather_far(0)
    gather_plane(2)
    swap_out.wait_recv()
    w_out_t[1] = w_out_ref[1].T
    swap_in.wait_recv()
    w_in_t[1] = w_in_ref[1].T
    gather_far(1)
    gather_end(0)
    compute(0)
    scatter_plane(0)
    gather_far(2)
    gather_end(1)
    compute(1)
    scatter_plane(1)
    scatter_near(0)
    gather_end(2)
    compute(2)
    scatter_plane(2)
    scatter_z(0)
    scatter_near(1)
    their_weights()
    scatter_near(2)
    scatter_z(1)
    own_weights()
    scatter_z(2)
    swaps[2].wait_recv()
    for tile in range(tiles):
        for side in range(2):
            left = side * half + tile * 128
            where = pl.ds(tile * 2 + side, width, stride=2 * tiles)
            grad_in_ref[where, :] = grad_in_ref[where, :] + take_in[
                :, left : left + 128
            ].astype(jnp.float32)
    swaps[3].wait_recv()
    grad_out_ref[...] = grad_out_ref[...] + take_out[...].astype(jnp.float32)
    last = len(sent) - 6
    for g in range(batches):
        if g == batches - 1:
            for copy in sent[:last]:
                copy.wait_send()
        scatter_end(g)
    total_mixed = jnp.concatenate(totals[0], axis=0)
    mixed_ref[...] = total_mixed[:, :width].astype(jnp.bfloat16)
    grad_tok_ref[...] = jnp.concatenate(totals[1], axis=0).astype(jnp.bfloat16)
    by_expert = total_mixed[:, width:]
    lines = []
    for k in range(per_token):
        chosen = jnp.logical_and(ids[k] == col_expert, col < 2 * groups)
        value = jnp.sum(jnp.where(chosen, by_expert, 0.0), axis=1, keepdims=True)
        lines.append(jnp.sum(jnp.where(diagonal, value, 0.0), axis=0, keepdims=True))
    grad_gates_ref[...] = jnp.concatenate(lines, axis=0)
    for copy in swaps + sent[last:]:
        copy.wait_send()


def dense_plan(tokens, grad_out, expert_ids, gates, w_in, w_out):
    count, width = tokens.shape
    groups = lax.axis_size("expert")
    half = w_out.shape[1]
    devices = 2 * groups
    batch = 8
    batches = count // batch
    vmem = pl.BlockSpec(memory_space=pltpu.VMEM)
    anywhere = pl.BlockSpec(memory_space=pl.ANY)
    total_rows = devices * count
    wide = width + GATE_COLS
    tiles = half // 128
    outs = pl.pallas_call(
        functools.partial(moe_kernel, groups),
        out_shape=(
            jax.ShapeDtypeStruct((count, width), jnp.bfloat16),
            jax.ShapeDtypeStruct((count, width), jnp.bfloat16),
            jax.ShapeDtypeStruct(gates.shape[::-1], jnp.float32),
            jax.ShapeDtypeStruct((width * 2 * tiles, 128), jnp.float32),
            jax.ShapeDtypeStruct((half, width), jnp.float32),
        ),
        in_specs=[vmem] * 4 + [anywhere] * 2,
        out_specs=[vmem] * 5,
        scratch_shapes=[
            pltpu.VMEM((batches, groups, batch, wide), jnp.bfloat16),
            pltpu.VMEM((batches, groups, batch, width), jnp.bfloat16),
            pltpu.VMEM((batches, groups, batch, wide), jnp.bfloat16),
            pltpu.VMEM((batches, groups, batch, width), jnp.bfloat16),
            pltpu.VMEM((batches, devices, batch, wide), jnp.bfloat16),
            pltpu.VMEM((batches, devices, batch, width), jnp.bfloat16),
            pltpu.VMEM((total_rows // 2, width), jnp.bfloat16),
            pltpu.VMEM((total_rows // 2, width), jnp.bfloat16),
            pltpu.VMEM((2, total_rows // 2, half), jnp.bfloat16),
            pltpu.VMEM((2, total_rows // 2, 2 * half), jnp.bfloat16),
            pltpu.VMEM((2, width, 2 * half), jnp.bfloat16),
            pltpu.VMEM((2, half, width), jnp.bfloat16),
            pltpu.VMEM((2, 2 * half, width), jnp.bfloat16),
            pltpu.VMEM((2, width, half), jnp.bfloat16),
            pltpu.VMEM((width, 2 * half), jnp.bfloat16),
            pltpu.VMEM((half, width), jnp.bfloat16),
            pltpu.VMEM((width, 2 * half), jnp.bfloat16),
            pltpu.VMEM((half, width), jnp.bfloat16),
            pltpu.SemaphoreType.DMA((batches, 2, devices)),
            pltpu.SemaphoreType.DMA((batches, 2, devices)),
            pltpu.SemaphoreType.DMA((batches, 2, devices)),
            pltpu.SemaphoreType.DMA((batches, 2, devices)),
            pltpu.SemaphoreType.DMA((2,)),
            pltpu.SemaphoreType.DMA((4,)),
            pltpu.SemaphoreType.DMA((4,)),
        ],
        compiler_params=pltpu.CompilerParams(
            collective_id=0, has_side_effects=True, vmem_limit_bytes=44 * 1024 * 1024
        ),
        cost_estimate=pl.CostEstimate(
            flops=18 * total_rows * width * half,
            bytes_accessed=12 * width * half + 6 * width * half,
            transcendentals=total_rows * half,
        ),
    )(tokens, grad_out, expert_ids.T, gates.T, w_in.reshape(width, 2 * half), w_out[0])
    mixed, grad_tokens, grad_gates, grad_in, grad_out_w = outs
    grad_in = grad_in.reshape(width, tiles, 2, 128).transpose(0, 2, 1, 3).reshape(w_in.shape)
    return (mixed, grad_tokens, grad_gates.T, grad_in, grad_out_w[None])


def per_device(tokens, grad_out, expert_ids, gates, w_in, w_out):
    if lax.axis_size("expert") == 16 and lax.axis_size("dp") == 2:
        return dense_plan(tokens, grad_out, expert_ids, gates, w_in, w_out)
    return routed_plan(tokens, grad_out, expert_ids, gates, w_in, w_out)


def solution(mesh):
    in_specs = (
        P(("dp", "expert"), None),
        P(("dp", "expert"), None),
        P(("dp", "expert"), None),
        P(("dp", "expert"), None),
        P("expert", None, None, "dp"),
        P("expert", "dp", None),
    )
    out_specs = (
        P(("dp", "expert"), None),
        P(("dp", "expert"), None),
        P(("dp", "expert"), None),
        P("expert", None, None, "dp"),
        P("expert", "dp", None),
    )
    return jax.shard_map(
        per_device, mesh=mesh, in_specs=in_specs, out_specs=out_specs, check_vma=False
    )
```
